256 devices in a mesh: seq: 64 (over z, x, core), head: 4 (over y).
Axes of the slice: x: 4, y: 4, z: 8, core: 2. Of those that a mesh axis runs over, the one named last changes fastest.
Arguments:
- states: bfloat16 [32768, 2048], P('seq'), may hold values from -6 to 6
- inner_weight: bfloat16 [2048, 4096], P(None, 'head'), may hold values from -0.125 to 0.125
- gate_weight: bfloat16 [2048, 4096], P(None, 'head'), may hold values from -1 to 1
- state_weight: bfloat16 [2048, 256], replicated, may hold values from -0.125 to 0.125
- step_weight: bfloat16 [2048, 32], P(None, 'head'), may hold values from -0.125 to 0.125
- step_bias: float32 [32], P('head'), may hold values from -4 to -2
- decay_rate: float32 [32], P('head'), may hold values from 0 to 1
- skip_gain: float32 [32], P('head'), may hold values from 0.5 to 1.5
- conv_inner: float32 [4, 4096], P(None, 'head'), may hold values from -3 to 3
- conv_state: float32 [4, 256], replicated, may hold values from -3 to 3
- norm_gain: float32 [4096], P('head'), may hold values from 0.5 to 2
- value_weight: float32 [4096], P('head'), may hold values from -0.09375 to 0.09375
- rewards: float32 [32768], P('seq'), may hold values from -4 to 4
- done_flags: int32 [32768], P('seq'), may hold values from 0 to 1, as said below
- horizon: int32 [32768], P('seq'), may hold values from 1 to 8
Outputs:
- values: float32 [32768], P('seq')
- targets: float32 [32768], P('seq')
- value_loss: float32 [], replicated
The draws below stay inside these ranges and needn't reach their ends.
Inputs may be any that keep to these rules, and one draw needn't show every extreme that they name: `done_flags`: exactly one time step of the trajectory has an episode end.
All inputs are finite; a program needn't handle non-finite values.
Results may differ from the reference program's by a relative error of at most 0.007.
Values may be sent and summed in bfloat16 or wider, within the bound.
A program may use at most 128 MiB of HBM per device.

```python
import math
import jax
import jax.numpy as jnp
from jax import lax

D = 2048
D_INNER = 4096
HEADS = 32
STATE = 128
KCONV = 4
NSTEP = 8
HDIM = 128
SEQ_LEN = 32768


def draw_gate_weight(key, part):
    column = jnp.arange(D_INNER, dtype=jnp.float32) / (D_INNER - 1)
    noise = jnp.clip(jax.random.normal(key, (D, D_INNER), jnp.float32), -4.0, 4.0)
    scales = 0.4 * 10.0 ** column
    return jnp.clip(noise * scales[None, :] / math.sqrt(D), -1.0, 1.0).astype(jnp.bfloat16)


def draw_decay_rate(key, part):
    order_key, slow_key, fast_key = jax.random.split(key, 3)
    ranking = jax.random.permutation(order_key, HEADS)
    slow_count = HEADS // 2
    slow_rate = jnp.exp(jax.random.uniform(slow_key, (HEADS,), jnp.float32, math.log(0.3), math.log(1.5))) / (0.1 * SEQ_LEN)
    fast_rate = jnp.exp(jax.random.uniform(fast_key, (HEADS,), jnp.float32, math.log(0.05), math.log(0.6)))
    return jnp.where(ranking < slow_count, slow_rate, fast_rate)


def draw_rewards(key, part):
    ramp = 1.0 + 2.0 * jnp.arange(SEQ_LEN, dtype=jnp.float32) / (SEQ_LEN - 1)
    noise = 0.2 * jnp.clip(jax.random.normal(key, (SEQ_LEN,), jnp.float32), -4.0, 4.0)
    return noise * ramp


def draw_done_flags(key, part):
    flag_key = jax.random.fold_in(key, 7)
    spread = max(1, 2 ** 30 // SEQ_LEN)
    scores = jax.random.randint(flag_key, (SEQ_LEN,), 0, spread, jnp.int32) * SEQ_LEN + jnp.arange(SEQ_LEN, dtype=jnp.int32)
    return (scores == jnp.max(scores)).astype(jnp.int32)


def touch_ends(result, key, low, largest):
    longest = result.shape.index(max(result.shape))
    spots = []
    for shift in (0, 1):
        where = [jax.random.randint(jax.random.fold_in(key, axis), (), 0, length) for axis, length in enumerate(result.shape)]
        where[longest] = (where[longest] + shift) % result.shape[longest]
        spots.append(tuple(where))
    return result.at[spots[0]].set(low).at[spots[1]].set(largest)


def block_levels(stream_key, extent, shards, low, largest):
    def one(axis_at, shards_of):
        draws = jax.random.uniform(jax.random.fold_in(jax.random.fold_in(stream_key, 6), axis_at), (shards_of,), jnp.float32, low / len(shards), largest / len(shards))
        return jnp.repeat(jnp.exp(draws), extent[axis_at] // shards_of).reshape((-1,) + (1,) * (len(extent) - axis_at - 1))

    factor_of = one(*shards[0])
    for cut in shards[1:]:
        factor_of = factor_of * one(*cut)
    return factor_of


def centred(stream_key, extent, width, limit, cuts=(), kind=jnp.bfloat16):
    result = jax.random.normal(stream_key, extent, jnp.float32) * width
    if len(cuts) > 0:
        result = block_levels(stream_key, extent, cuts, -0.22, 0.18) * result
    return jnp.clip(result, min=-limit, max=limit).astype(kind)


def setup_inputs(seed: int = 0) -> dict:
    keys = jax.random.split(jax.random.key(seed), 16)
    return {
        "states": centred(keys[0], (SEQ_LEN, D), 1.0, 6.0, ((0, 64),)),
        "inner_weight": centred(keys[1], (D, D_INNER), D ** -0.5, 0.125, ((1, 4),)),
        "gate_weight": draw_gate_weight(jax.random.fold_in(keys[15], 71), 0),
        "state_weight": centred(keys[3], (D, 2 * STATE), D ** -0.5, 0.125),
        "step_weight": centred(keys[4], (D, HEADS), D ** -0.5, 0.125, ((1, 4),)),
        "step_bias": jnp.clip(-4.0 + 2.0 * jax.random.uniform(keys[5], (HEADS,), jnp.float32) ** block_levels(keys[5], (HEADS,), ((0, 4),), -0.2, 0.2), -4.0, -2.0),
        "decay_rate": draw_decay_rate(jax.random.fold_in(keys[15], 71), 0),
        "skip_gain": jnp.clip(0.5 + 1.0 * jax.random.uniform(keys[7], (HEADS,), jnp.float32) ** block_levels(keys[7], (HEADS,), ((0, 4),), -0.2, 0.2), 0.5, 1.5),
        "conv_inner": centred(keys[8], (KCONV, D_INNER), KCONV ** -0.5, 3.0, ((1, 4),), jnp.float32),
        "conv_state": centred(keys[9], (KCONV, 2 * STATE), KCONV ** -0.5, 3.0, (), jnp.float32),
        "norm_gain": jnp.clip(jnp.exp(math.log(2.0) - 1.3862944 * jax.random.uniform(keys[10], (D_INNER,), jnp.float32) ** block_levels(keys[10], (D_INNER,), ((0, 4),), -0.2, 0.2)), 0.5, 2.0),
        "value_weight": centred(keys[11], (D_INNER,), D_INNER ** -0.5, 0.09375, ((0, 4),), jnp.float32),
        "rewards": draw_rewards(jax.random.fold_in(keys[15], 71), 0),
        "done_flags": draw_done_flags(jax.random.fold_in(keys[15], 71), 0),
        "horizon": touch_ends(jax.random.randint(keys[14], (SEQ_LEN,), 1, NSTEP + 1), jax.random.fold_in(keys[14], 1), 1, NSTEP).astype(jnp.int32),
    }


DISCOUNT = 0.99
EXPECTILE = 0.7
EPSILON = 1e-05

def causal_conv(rim_rows, projected, kernel):
    padded = jnp.concatenate([rim_rows.astype(jnp.float32), projected.astype(jnp.float32)], axis=0)
    length = projected.shape[0]
    summed = jnp.zeros(projected.shape, jnp.float32)
    for offset in range(kernel.shape[0]):
        summed = summed + kernel[offset] * padded[offset:offset + length]
    return jax.nn.silu(summed).astype(jnp.bfloat16)

def block_scan(inner, writes, readout, step_size, decay_rate, done_int, running_state):
    precise = lax.Precision.HIGHEST
    inputs = step_size[:, :, None] * inner.astype(jnp.float32)
    local_decay = jnp.cumsum(-decay_rate * step_size, axis=0)
    done_count = jnp.cumsum(done_int)
    done_before = done_count - done_int
    scores = jnp.dot(readout, writes.T, preferred_element_type=jnp.float32)
    positions = jnp.arange(inner.shape[0])
    causal_mask = (positions[:, None] >= positions[None, :]) & (done_before[:, None] == done_before[None, :])
    decay_gap = local_decay[:, None, :] - local_decay[None, :, :]
    weights = scores[:, :, None] * jnp.exp(jnp.where(causal_mask[:, :, None], decay_gap, -jnp.inf))
    block_out = jnp.einsum('tsh,shp->thp', weights, inputs, precision=precise)
    carry_reach = jnp.exp(local_decay) * (done_before == 0)[:, None]
    readout_float = readout.astype(jnp.float32)
    block_out = block_out + carry_reach[:, :, None] * jnp.einsum('tn,hpn->thp', readout_float, running_state, precision=precise)
    tail_weight = jnp.exp(local_decay[-1][None, :] - local_decay) * (done_count[-1] - done_before == 0)[:, None]
    block_state = jnp.einsum('shp,sn->hpn', tail_weight[:, :, None] * inputs, writes.astype(jnp.float32), precision=precise)
    block_decay = jnp.exp(local_decay[-1]) * (done_count[-1] == 0)
    return (block_out, block_decay[:, None, None] * running_state + block_state, block_decay)

def nstep_targets(reward_ext, alive_ext, value_ext, horizon, length):
    targets = jnp.zeros((length,), jnp.float32)
    survive = jnp.ones((length,), jnp.float32)
    for offset in range(NSTEP + 1):
        factor = DISCOUNT ** offset * survive
        targets = targets + jnp.where(offset < horizon, factor * reward_ext[offset:offset + length], 0.0)
        targets = targets + jnp.where(offset == horizon, factor * value_ext[offset:offset + length], 0.0)
        survive = survive * alive_ext[offset:offset + length]
    return targets

def expectile_terms(targets, values):
    residual = targets - values
    return jnp.where(residual < 0, 1.0 - EXPECTILE, EXPECTILE) * residual * residual

def reference(states, inner_weight, gate_weight, state_weight, step_weight, step_bias, decay_rate, skip_gain, conv_inner, conv_state, norm_gain, value_weight, rewards, done_flags, horizon):
    inner_pre = jnp.dot(states, inner_weight, preferred_element_type=jnp.float32).astype(jnp.bfloat16)
    gate_pre = jnp.dot(states, gate_weight, preferred_element_type=jnp.float32).astype(jnp.bfloat16)
    state_pre = jnp.dot(states, state_weight, preferred_element_type=jnp.float32).astype(jnp.bfloat16)
    step_size = jax.nn.softplus(jnp.dot(states, step_weight, preferred_element_type=jnp.float32) + step_bias)
    block_size = math.gcd(SEQ_LEN, 256)
    conv_lag = KCONV - 1

    def advance(carry, block_index):
        running_state, inner_rim, state_rim = carry
        start_row = (block_index * block_size).astype(jnp.int32)
        inner_rows = lax.dynamic_slice_in_dim(inner_pre, start_row, block_size, 0)
        gate_rows = lax.dynamic_slice_in_dim(gate_pre, start_row, block_size, 0)
        state_rows = lax.dynamic_slice_in_dim(state_pre, start_row, block_size, 0)
        step_rows = lax.dynamic_slice_in_dim(step_size, start_row, block_size, 0)
        done_rows = lax.dynamic_slice_in_dim(done_flags, start_row, block_size, 0)
        inner_conv = causal_conv(inner_rim, inner_rows, conv_inner)
        state_conv = causal_conv(state_rim, state_rows, conv_state)
        inner_heads = inner_conv.reshape(block_size, HEADS, HDIM)
        block_out, running_state, unused = block_scan(inner_heads, state_conv[:, :STATE], state_conv[:, STATE:], step_rows, decay_rate, done_rows, running_state)
        mixed_heads = block_out + skip_gain[None, :, None] * inner_heads.astype(jnp.float32)
        gated = mixed_heads.reshape(block_size, D_INNER) * jax.nn.silu(gate_rows.astype(jnp.float32))
        square_sum = lax.optimization_barrier(jnp.sum(gated * gated, axis=1))
        normed = gated * lax.rsqrt(square_sum / D_INNER + EPSILON)[:, None] * norm_gain
        block_values = lax.optimization_barrier(jnp.sum(normed * value_weight, axis=1))
        return ((running_state, inner_rows[block_size - conv_lag:], state_rows[block_size - conv_lag:]), block_values)
    initial = (jnp.zeros((HEADS, HDIM, STATE), jnp.float32), jnp.zeros((conv_lag, D_INNER), jnp.bfloat16), jnp.zeros((conv_lag, 2 * STATE), jnp.bfloat16))
    unused, values = lax.scan(advance, initial, jnp.arange(SEQ_LEN // block_size, dtype=jnp.int32))
    values = values.reshape(SEQ_LEN)
    padding = jnp.zeros((NSTEP,), jnp.float32)
    alive = 1.0 - done_flags.astype(jnp.float32)
    targets = nstep_targets(jnp.concatenate([rewards, padding]), jnp.concatenate([alive, padding]), jnp.concatenate([values, padding]), horizon, SEQ_LEN)
    value_loss = jnp.sum(expectile_terms(targets, values)) / SEQ_LEN
    return (values, targets, value_loss)
```

```python
import functools

import jax
import jax.numpy as jnp
from jax import lax
from jax.experimental import pallas as pl
from jax.experimental.pallas import tpu as pltpu
from jax.sharding import Mesh
from jax.sharding import PartitionSpec as P

SEQ = ("seq_0", "seq_1", "seq_2")
MESH = pl.DeviceIdType.MESH
F32 = jnp.float32
BF16 = jnp.bfloat16

KCONV = 4
NSTEP = 8
DISCOUNT = 0.99
EXPECTILE = 0.7
EPSILON = 1e-05

HALO = 16
ROWS = 512
DEPTH = 2048
HEADS = 8
LANES = 128
WIDE = 256
TILES = HEADS * LANES // WIDE
PLANE = 8
DEPTHS = 8
PEERS = 4


def silu(value):
    half = 0.5 * value
    return half + half * jnp.tanh(half)


def dot(a, b):
    return jnp.dot(a, b, preferred_element_type=F32)


def three_pieces(value):
    high = value.astype(BF16).astype(F32)
    rest = value - high
    middle = rest.astype(BF16).astype(F32)
    return high, middle, rest - middle


def decay_rows(row):
    high, middle, low = three_pieces(row)
    place = lax.broadcasted_iota(jnp.int32, (16, LANES), 0)
    rows = jnp.where(place == 0, high, 0.0)
    rows = jnp.where(place == 1, middle, rows)
    return jnp.where(place == 2, low, rows).astype(BF16)


def down(row, rows=LANES):
    return jnp.broadcast_to(row, (rows, row.shape[1])).T


def kernel(
    seq_total,
    states,
    w_in,
    w_gate,
    w_state,
    w_step,
    bias,
    rate,
    skip,
    taps_in,
    taps_st,
    gain,
    weight,
    rewards,
    done,
    horizon,
    values_out,
    targets_out,
    loss_out,
    xs,
    wi,
    wg,
    ws,
    wt_in,
    wt,
    tin,
    tst,
    gn,
    vw,
    rw,
    dn,
    hz,
    pre,
    xh,
    rdm,
    wtf,
    sc,
    lrow,
    dtrow,
    tail,
    decb,
    y,
    gs,
    rs,
    send1,
    recv1,
    inside,
    reach_in,
    send2,
    recv2,
    send3,
    recv3,
    send4,
    recv4,
    part,
    recvh,
    recvn,
    ext,
    recvr,
    coef,
    loss1,
    recvl1,
    loss2,
    recvl2,
    local_sem,
    tile_sem,
    halo_sem,
    s1,
    r1,
    s2,
    r2,
    s3,
    r3,
    s4,
    r4,
    sh,
    rh,
    sn,
    rn,
    sl1,
    rl1,
    sl2,
    rl2,
):
    z, x, c, head = (lax.axis_index(name) for name in SEQ + ("head",))
    here = x * 2 + c
    place = z * PLANE + here
    total = DEPTHS * PLANE
    after = lax.rem(place + 1, total)
    before = lax.rem(place + total - 1, total)

    def of_place(at, at_head):
        return (lax.div(at, PLANE), lax.div(lax.rem(at, PLANE), 2), lax.rem(at, 2), at_head)

    def in_plane(q):
        return (z, lax.div(q, 2), lax.rem(q, 2), head)

    def in_depth(k):
        return (k, x, c, head)

    def in_head(k):
        return (z, x, c, k)

    def put(src, dst, ssem, rsem, device):
        return pltpu.make_async_remote_copy(
            src_ref=src, dst_ref=dst, send_sem=ssem, recv_sem=rsem, device_id=device, device_id_type=MESH
        )

    def others(me, count, act):
        def one(i, carry):
            act(lax.rem(me + i, count))
            return carry

        lax.fori_loop(1, count, one, 0)

    small = [
        (states, xs.at[pl.ds(HALO, ROWS), :]),
        (w_step, wt_in),
        (w_state, ws),
        (taps_st, tst),
        (taps_in, tin),
        (done, dn),
        (rewards, rw),
        (gain, gn),
        (weight, vw),
        (horizon, hz),
    ]
    local = [pltpu.make_async_copy(src, dst, local_sem.at[i]) for i, (src, dst) in enumerate(small)]

    def tile_copy(src, dst, slot, which):
        columns = pl.ds(pl.multiple_of(which * WIDE, WIDE), WIDE)
        return pltpu.make_async_copy(src.at[:, columns], dst.at[which], tile_sem.at[slot, which])

    def turned(j):
        return lax.rem(j + x, TILES)

    for copy in local[:3]:
        copy.start()
    for copy in local[3:]:
        copy.start()
    for j in range(TILES):
        tile_copy(w_in, wi, 0, turned(j)).start()
    for j in range(TILES):
        tile_copy(w_gate, wg, 1, j).start()

    barrier = pltpu.get_barrier_semaphore()

    def greet(device):
        pl.semaphore_signal(barrier, inc=1, device_id=device, device_id_type=MESH)

    others(here, PLANE, lambda q: greet(in_plane(q)))
    others(z, DEPTHS, lambda k: greet(in_depth(k)))
    others(head, PEERS, lambda k: greet(in_head(k)))
    greet(of_place(before, head))
    for k in range(PEERS):
        greet(of_place(after, k))
    pl.semaphore_wait(barrier, (PLANE - 1) + (DEPTHS - 1) + (PEERS - 1) + 1 + PEERS)

    halo = put(
        states.at[pl.ds(ROWS - HALO, HALO), :],
        xs.at[pl.ds(0, HALO), :],
        halo_sem.at[0],
        halo_sem.at[1],
        of_place(after, head),
    )
    halo.start()

    local[5].wait()
    local[6].wait()
    alive = 1.0 - dn[...].astype(F32)
    ext[...] = jnp.zeros((8, ROWS + LANES), F32)
    ext[0:1, 0:ROWS] = rw[...]
    ext[1:2, 0:ROWS] = alive
    rim = put(
        ext.at[:, pl.ds(0, LANES)], recvr, halo_sem.at[2], halo_sem.at[3], of_place(before, head)
    )
    rim.start()
    part[...] = jnp.zeros((8, ROWS), F32)

    local[0].wait()
    local[1].wait()
    wt[...] = jnp.concatenate(
        [wt_in[...].astype(F32), jnp.zeros((LANES - HEADS, DEPTH), F32)], axis=0
    ).astype(BF16)
    step_pre = lax.dot_general(
        xs[HALO : HALO + ROWS, :],
        wt[...],
        (((1,), (1,)), ((), ())),
        preferred_element_type=F32,
    ).T[0:HEADS, :]
    order = lax.broadcasted_iota(jnp.int32, (HEADS, ROWS), 0)
    bias_rows = jnp.zeros((HEADS, ROWS), F32)
    rate_rows = jnp.zeros((HEADS, ROWS), F32)
    for h in range(HEADS):
        bias_rows = jnp.where(order == h, bias[h], bias_rows)
        rate_rows = jnp.where(order == h, rate[h], rate_rows)
    step_pre = step_pre + bias_rows
    step = jnp.maximum(step_pre, 0.0) + jnp.log1p(jnp.exp(-jnp.abs(step_pre)))
    dtrow[...] = step
    done_rows = jnp.broadcast_to(dn[...].astype(F32), (HEADS, ROWS))
    blocks = ROWS // LANES
    pieces = three_pieces(-(rate_rows * step)) + (done_rows,)
    stacked = jnp.concatenate(
        [p[:, b * LANES : (b + 1) * LANES] for p in pieces for b in range(blocks)], axis=0
    ).astype(BF16)
    triangle = (
        lax.broadcasted_iota(jnp.int32, (LANES, LANES), 0)
        <= lax.broadcasted_iota(jnp.int32, (LANES, LANES), 1)
    ).astype(F32).astype(BF16)
    sums = dot(stacked, triangle)
    span = HEADS * blocks
    decays = sums[0:span] + sums[span : 2 * span] + sums[2 * span : 3 * span]
    dones = sums[3 * span : 4 * span]

    def joined(parts):
        found, offset = [], jnp.zeros((HEADS, 1), F32)
        for b in range(blocks):
            block = parts[b * HEADS : (b + 1) * HEADS, :] + offset
            offset = block[:, LANES - 1 : LANES]
            found.append(block)
        return jnp.concatenate(found, axis=1), offset

    running, last = joined(decays)
    done_to, done_all = joined(dones)
    done_before = done_to - done_rows
    lrow[...] = running
    tail[...] = jnp.where(done_before == done_all, jnp.exp(last - running) * step, 0.0)
    decb[...] = jnp.broadcast_to(jnp.where(done_all == 0.0, jnp.exp(last), 0.0), (HEADS, LANES))
    done_row = done_before[0:1, :]
    done_down = down(done_row)

    local[2].wait()
    local[3].wait()
    halo.wait_recv()
    inner_edge = jnp.where(place > 0, 1.0, 0.0)

    def convolved(taps):
        whole = pre[HALO : HALO + ROWS, :] * taps[KCONV - 1 : KCONV, :]
        for k in range(KCONV - 1):
            lag = KCONV - 1 - k
            whole = whole + pre[HALO - lag : HALO - lag + ROWS, :] * taps[k : k + 1, :]
        return silu(whole)

    pre[...] = dot(xs[...], ws[...])
    pre[0:HALO, :] = pre[0:HALO, :] * inner_edge
    state_conv = convolved(tst[...])
    wtf[...] = state_conv[:, 0:LANES].T
    writes_t = wtf[...].astype(BF16)
    readout = state_conv[:, LANES:WIDE]
    rdm[...] = jnp.where(done_down == 0.0, readout, 0.0)
    readout = readout.astype(BF16)
    for b in range(2):
        rows = slice(b * WIDE, (b + 1) * WIDE)
        upto = (b + 1) * WIDE
        scores = dot(readout[rows, :], writes_t[:, 0:upto])
        at_row = lax.broadcasted_iota(jnp.int32, (WIDE, LANES), 0) + b * WIDE
        for k in range(upto // LANES):
            columns = slice(k * LANES, (k + 1) * LANES)
            at_column = lax.broadcasted_iota(jnp.int32, (WIDE, LANES), 1) + k * LANES
            seen = (at_row >= at_column) & (done_down[rows, :] == done_row[:, columns])
            sc[rows, columns] = jnp.where(seen, scores[:, columns], 0.0)

    local[4].wait()

    def inner_tile(j, carry):
        which = turned(j)
        tile_copy(w_in, wi, 0, which).wait()
        pre[...] = dot(xs[...], wi[which])
        pre[0:HALO, :] = pre[0:HALO, :] * inner_edge
        taps = tin[:, pl.ds(pl.multiple_of(which * WIDE, WIDE), WIDE)]
        conv = convolved(taps).astype(BF16)
        for k in range(2):
            h = which * 2 + k
            inner = conv[:, k * LANES : (k + 1) * LANES]
            xh[h] = inner
            gained = dot((wtf[...] * tail[pl.ds(h, 1), :]).astype(BF16), inner).astype(BF16)
            lost = decay_rows(decb[pl.ds(h, 1), :])

            @pl.when(h == here)
            def _():
                recv1[h, 0:LANES, :] = gained
                recv1[h, LANES : LANES + 16, :] = lost

            @pl.when(h != here)
            def _():
                send1[h, 0:LANES, :] = gained
                send1[h, LANES : LANES + 16, :] = lost
                put(send1.at[h], recv1.at[here], s1.at[h], r1.at[here], in_plane(h)).start()

        return carry

    lax.fori_loop(0, TILES, inner_tile, 0)

    def gate_tile(j, carry):
        tile_copy(w_gate, wg, 1, j).wait()
        gate = silu(dot(xs[HALO : HALO + ROWS, :], wg[j]))
        for k in range(2):
            gs[j * 2 + k] = gate[:, k * LANES : (k + 1) * LANES]
        return carry

    lax.fori_loop(0, TILES // 2, gate_tile, 0)

    others(here, PLANE, lambda q: put(send1.at[q], recv1.at[q], s1.at[q], r1.at[q], in_plane(q)).wait_recv())

    def plane_step(q, carry):
        state, lasting = carry
        inside[q] = state
        reach_in[q] = jnp.broadcast_to(lasting, (8, LANES))
        lost = jnp.sum(recv1[q, LANES : LANES + 16, :].astype(F32), axis=0, keepdims=True)
        return lost * state + recv1[q, 0:LANES, :].astype(F32), lasting * lost

    state, lasting = lax.fori_loop(
        0, PLANE, plane_step, (jnp.zeros((LANES, LANES), F32), jnp.ones((1, LANES), F32))
    )
    send2[:, 0:16, :] = state.astype(BF16).reshape(DEPTHS, 16, LANES)
    send2[:, 16:32, :] = jnp.broadcast_to(decay_rows(lasting)[None], (DEPTHS, 16, LANES))
    recv2[z] = send2[z]
    others(z, DEPTHS, lambda k: put(send2.at[k], recv2.at[z], s2.at[k], r2.at[z], in_depth(k)).start())

    lax.fori_loop(TILES // 2, TILES, gate_tile, 0)

    others(z, DEPTHS, lambda k: put(send2.at[k], recv2.at[k], s2.at[k], r2.at[k], in_depth(k)).wait_recv())

    def depth_step(k, state):
        send3[k] = state.astype(BF16)
        lost = jnp.sum(recv2[k, 16:32, :].astype(F32), axis=0, keepdims=True)
        return lost * state + recv2[k, 0:16, :].astype(F32)

    lax.fori_loop(0, DEPTHS, depth_step, jnp.zeros((16, LANES), F32))
    recv3[z] = send3[z]
    others(z, DEPTHS, lambda k: put(send3.at[k], recv3.at[z], s3.at[k], r3.at[z], in_depth(k)).start())

    def own_scan(h, carry):
        across = lrow[pl.ds(h, 1), :]
        step_across = dtrow[pl.ds(h, 1), :]
        along = down(across)
        inner = xh[h]
        for b in range(2):
            rows = slice(b * WIDE, (b + 1) * WIDE)
            upto = (b + 1) * WIDE
            weights = []
            for k in range(upto // LANES):
                columns = slice(k * LANES, (k + 1) * LANES)
                gap = jnp.minimum(along[rows, :] - across[:, columns], 0.0)
                weights.append((jnp.exp(gap) * step_across[:, columns] * sc[rows, columns]).astype(BF16))
            mixed = dot(jnp.concatenate(weights, axis=1), inner[0:upto, :])
            y[h, rows, :] = mixed + skip[h] * inner[rows, :].astype(F32)
        rs[h] = (rdm[...] * jnp.exp(along)).astype(BF16)
        return carry

    lax.fori_loop(0, HEADS // 2, own_scan, 0)

    others(z, DEPTHS, lambda k: put(send3.at[k], recv3.at[k], s3.at[k], r3.at[k], in_depth(k)).wait_recv())
    entering = recv3[...].astype(F32).reshape(LANES, LANES)

    def hand_out(i, carry):
        q = lax.rem(here + i, PLANE)
        carried = (reach_in[q][0:1, :] * entering + inside[q]).astype(BF16)

        @pl.when(q == here)
        def _():
            recv4[q] = carried

        @pl.when(q != here)
        def _():
            send4[q] = carried
            put(send4.at[q], recv4.at[here], s4.at[q], r4.at[here], in_plane(q)).start()

        return carry

    lax.fori_loop(0, PLANE, hand_out, 0)

    lax.fori_loop(HEADS // 2, HEADS, own_scan, 0)

    local[7].wait()
    local[8].wait()
    local[9].wait()
    rim.wait_recv()
    is_last = place == total - 1
    ext[:, ROWS : ROWS + LANES] = jnp.where(is_last, 0.0, recvr[...])
    length = ROWS + LANES
    survive = jnp.ones((1, ROWS), F32)
    rewarded = jnp.zeros((1, ROWS), F32)
    for k in range(NSTEP + 1):
        ahead = ext[...] if k == 0 else pltpu.roll(ext[...], length - k, 1)
        factor = DISCOUNT**k * survive
        rewarded = rewarded + jnp.where(k < hz[...], factor * ahead[0:1, 0:ROWS], 0.0)
        coef[k : k + 1, :] = jnp.where(k == hz[...], factor, 0.0)
        survive = survive * ahead[1:2, 0:ROWS]
    coef[NSTEP + 1 : NSTEP + 2, :] = rewarded
    gn[...] = gn[...] * vw[...]

    others(here, PLANE, lambda q: put(send4.at[q], recv4.at[q], s4.at[q], r4.at[q], in_plane(q)).wait_recv())

    def mix(b, carry):
        rows = pl.ds(pl.multiple_of(b * LANES, LANES), LANES)
        squares = jnp.zeros((LANES, LANES), F32)
        valued = jnp.zeros((LANES, LANES), F32)
        for h in range(HEADS):
            mixed = y[h, rows, :] + dot(rs[h, rows, :], recv4[h])
            gated = mixed * gs[h, rows, :]
            squares = squares + gated * gated
            valued = valued + gated * gn[:, h * LANES : (h + 1) * LANES]
        part[0:1, rows] = jnp.sum(squares.T, axis=0, keepdims=True)
        part[1:2, rows] = jnp.sum(valued.T, axis=0, keepdims=True)
        return carry

    lax.fori_loop(0, ROWS // LANES, mix, 0)

    def to_peer(k):
        return put(part, recvh.at[head], sh.at[k], rh.at[head], in_head(k))

    def to_before(k):
        return put(
            part.at[:, pl.ds(0, LANES)], recvn.at[head], sn.at[k], rn.at[head], of_place(before, k)
        )

    others(head, PEERS, lambda k: to_peer(k).start())
    for k in range(PEERS):
        to_before(k).start()
    recvh[head] = part[...]
    others(head, PEERS, lambda k: put(part, recvh.at[k], sh.at[k], rh.at[k], in_head(k)).wait_recv())
    for k in range(PEERS):
        put(part.at[:, pl.ds(0, LANES)], recvn.at[k], sn.at[k], rn.at[k], of_place(after, k)).wait_recv()

    def normed(sums):
        return sums[1:2, :] * lax.rsqrt(sums[0:1, :] / (PEERS * HEADS * LANES) + EPSILON)

    own = normed(recvh[0] + recvh[1] + recvh[2] + recvh[3])
    following = normed(recvn[0] + recvn[1] + recvn[2] + recvn[3])
    following = jnp.where(is_last, 0.0, following)
    valued = jnp.broadcast_to(jnp.concatenate([own, following], axis=1), (8, length))
    targets = coef[NSTEP + 1 : NSTEP + 2, :]
    for k in range(NSTEP + 1):
        ahead = valued if k == 0 else pltpu.roll(valued, length - k, 1)
        targets = targets + coef[k : k + 1, :] * ahead[0:1, 0:ROWS]
    values_out[...] = own
    targets_out[...] = targets
    residual = targets - own
    terms = jnp.where(residual < 0, 1.0 - EXPECTILE, EXPECTILE) * residual * residual
    loss1[...] = jnp.broadcast_to(jnp.sum(terms, axis=1, keepdims=True), (8, LANES))
    others(here, PLANE, lambda q: put(loss1, recvl1.at[here], sl1.at[q], rl1.at[here], in_plane(q)).start())
    recvl1[here] = loss1[...]
    others(here, PLANE, lambda q: put(loss1, recvl1.at[q], sl1.at[q], rl1.at[q], in_plane(q)).wait_recv())
    loss2[...] = jnp.sum(recvl1[...], axis=0)
    others(z, DEPTHS, lambda k: put(loss2, recvl2.at[z], sl2.at[k], rl2.at[z], in_depth(k)).start())
    recvl2[z] = loss2[...]
    others(z, DEPTHS, lambda k: put(loss2, recvl2.at[k], sl2.at[k], rl2.at[k], in_depth(k)).wait_recv())
    loss_out[...] = jnp.sum(recvl2[...], axis=0)[0:1, 0:1] / seq_total

    halo.wait_send()
    rim.wait_send()
    others(here, PLANE, lambda q: put(send1.at[q], recv1.at[q], s1.at[q], r1.at[q], in_plane(q)).wait_send())
    others(z, DEPTHS, lambda k: put(send2.at[k], recv2.at[k], s2.at[k], r2.at[k], in_depth(k)).wait_send())
    others(z, DEPTHS, lambda k: put(send3.at[k], recv3.at[k], s3.at[k], r3.at[k], in_depth(k)).wait_send())
    others(here, PLANE, lambda q: put(send4.at[q], recv4.at[q], s4.at[q], r4.at[q], in_plane(q)).wait_send())
    others(head, PEERS, lambda k: to_peer(k).wait_send())
    for k in range(PEERS):
        to_before(k).wait_send()
    others(here, PLANE, lambda q: put(loss1, recvl1.at[q], sl1.at[q], rl1.at[q], in_plane(q)).wait_send())
    others(z, DEPTHS, lambda k: put(loss2, recvl2.at[k], sl2.at[k], rl2.at[k], in_depth(k)).wait_send())


def scratch():
    v = pltpu.VMEM
    dma = pltpu.SemaphoreType.DMA
    return [
        v((HALO + ROWS, DEPTH), BF16),
        v((TILES, DEPTH, WIDE), BF16),
        v((TILES, DEPTH, WIDE), BF16),
        v((DEPTH, WIDE), BF16),
        v((HEADS, DEPTH), BF16),
        v((LANES, DEPTH), BF16),
        v((KCONV, HEADS * LANES), F32),
        v((KCONV, WIDE), F32),
        v((1, HEADS * LANES), F32),
        v((1, HEADS * LANES), F32),
        v((1, ROWS), F32),
        v((1, ROWS), jnp.int32),
        v((1, ROWS), jnp.int32),
        v((HALO + ROWS, WIDE), F32),
        v((HEADS, ROWS, LANES), BF16),
        v((ROWS, LANES), F32),
        v((LANES, ROWS), F32),
        v((ROWS, ROWS), F32),
        v((HEADS, ROWS), F32),
        v((HEADS, ROWS), F32),
        v((HEADS, ROWS), F32),
        v((HEADS, LANES), F32),
        v((HEADS, ROWS, LANES), F32),
        v((HEADS, ROWS, LANES), F32),
        v((HEADS, ROWS, LANES), BF16),
        v((PLANE, LANES + 16, LANES), BF16),
        v((PLANE, LANES + 16, LANES), BF16),
        v((PLANE, LANES, LANES), F32),
        v((PLANE, 8, LANES), F32),
        v((DEPTHS, 32, LANES), BF16),
        v((DEPTHS, 32, LANES), BF16),
        v((DEPTHS, 16, LANES), BF16),
        v((DEPTHS, 16, LANES), BF16),
        v((PLANE, LANES, LANES), BF16),
        v((PLANE, LANES, LANES), BF16),
        v((8, ROWS), F32),
        v((PEERS, 8, ROWS), F32),
        v((PEERS, 8, LANES), F32),
        v((8, ROWS + LANES), F32),
        v((8, LANES), F32),
        v((16, ROWS), F32),
        v((8, LANES), F32),
        v((PLANE, 8, LANES), F32),
        v((8, LANES), F32),
        v((DEPTHS, 8, LANES), F32),
        dma((10,)),
        dma((2, TILES)),
        dma((4,)),
        dma((PLANE,)),
        dma((PLANE,)),
        dma((DEPTHS,)),
        dma((DEPTHS,)),
        dma((DEPTHS,)),
        dma((DEPTHS,)),
        dma((PLANE,)),
        dma((PLANE,)),
        dma((PEERS,)),
        dma((PEERS,)),
        dma((PEERS,)),
        dma((PEERS,)),
        dma((PLANE,)),
        dma((PLANE,)),
        dma((DEPTHS,)),
        dma((DEPTHS,)),
    ]


def per_device(
    states,
    inner_weight,
    gate_weight,
    state_weight,
    step_weight,
    step_bias,
    decay_rate,
    skip_gain,
    conv_inner,
    conv_state,
    norm_gain,
    value_weight,
    rewards,
    done_flags,
    horizon,
):
    hbm = pl.BlockSpec(memory_space=pl.ANY)
    smem = pl.BlockSpec(memory_space=pltpu.SMEM)
    vmem = pl.BlockSpec(memory_space=pltpu.VMEM)
    seq_total = states.shape[0] * DEPTHS * PLANE
    values, targets, loss = pl.pallas_call(
        functools.partial(kernel, seq_total),
        out_shape=(
            jax.ShapeDtypeStruct((1, ROWS), F32),
            jax.ShapeDtypeStruct((1, ROWS), F32),
            jax.ShapeDtypeStruct((1, 1), F32),
        ),
        in_specs=[hbm] * 5 + [smem] * 3 + [hbm] * 7,
        out_specs=(vmem, vmem, vmem),
        scratch_shapes=scratch(),
        compiler_params=pltpu.CompilerParams(
            collective_id=0, has_side_effects=True, vmem_limit_bytes=56 * 2**20
        ),
    )(
        states,
        inner_weight,
        gate_weight,
        state_weight,
        step_weight.T,
        step_bias,
        decay_rate,
        skip_gain,
        conv_inner,
        conv_state,
        norm_gain.reshape(1, -1),
        value_weight.reshape(1, -1),
        rewards.reshape(1, -1),
        done_flags.reshape(1, -1),
        horizon.reshape(1, -1),
    )
    return values.reshape(-1), targets.reshape(-1), loss.reshape(())


def solution(mesh):
    torus = Mesh(
        mesh.devices.reshape(DEPTHS, 4, 2, mesh.shape["head"]), SEQ + ("head",)
    )
    placed = (
        P(SEQ, None),
        P(None, "head"),
        P(None, "head"),
        P(),
        P(None, "head"),
        P("head"),
        P("head"),
        P("head"),
        P(None, "head"),
        P(),
        P("head"),
        P("head"),
        P(SEQ),
        P(SEQ),
        P(SEQ),
    )
    return jax.shard_map(
        per_device, mesh=torus, in_specs=placed, out_specs=(P(SEQ), P(SEQ), P()), check_vma=False
    )
```

```python
import functools

import jax
import jax.numpy as jnp
from jax import lax
from jax.experimental import pallas as pl
from jax.experimental.pallas import tpu as pltpu
from jax.sharding import Mesh
from jax.sharding import PartitionSpec as P

SEQ = ("seq_0", "seq_1", "seq_2")
MESH = pl.DeviceIdType.MESH
F32 = jnp.float32
BF16 = jnp.bfloat16

KCONV = 4
NSTEP = 8
DISCOUNT = 0.99
EXPECTILE = 0.7
EPSILON = 1e-05

HALO = 16
ROWS = 512
HALF = 256
EARLY = 1
DEPTH = 2048
HEADS = 8
LANES = 128
WIDE = 256
TILES = HEADS * LANES // WIDE
PLANE = 8
DEPTHS = 8
PEERS = 4


def silu(value):
    half = 0.5 * value
    return half + half * jnp.tanh(half)


def dot(a, b):
    return jnp.dot(a, b, preferred_element_type=F32)


def three_pieces(value):
    high = value.astype(BF16).astype(F32)
    rest = value - high
    middle = rest.astype(BF16).astype(F32)
    return high, middle, rest - middle


def down(row, rows=LANES):
    return jnp.broadcast_to(row, (rows, row.shape[1])).T


def kernel(
    seq_total,
    states,
    w_in,
    w_gate,
    w_state,
    w_step,
    bias,
    rate,
    skip,
    taps_in,
    taps_st,
    gain,
    weight,
    rewards,
    done,
    horizon,
    out,
    xs,
    wi,
    wg,
    ws,
    wt_in,
    wt,
    tin,
    tst,
    gn,
    vw,
    rw,
    dn,
    hz,
    pre0,
    pre1,
    xh,
    ro,
    rdm,
    wtf,
    sc,
    lrow,
    dtrow,
    drow,
    tail,
    decb,
    recve1,
    dall,
    recve2,
    y,
    gs,
    rs,
    send1,
    recv1,
    inside,
    reach_in,
    send2,
    recv2,
    send4,
    recv4,
    part,
    recvh,
    recvn,
    ext,
    recvr,
    coef,
    loss1,
    recvl,
    local_sem,
    tile_sem,
    near_sem,
    send_sem,
    recv_sem,
    s2,
    r2,
):
    z, x, c, head = (lax.axis_index(name) for name in SEQ + ("head",))
    here = x * 2 + c
    place = z * PLANE + here
    total = DEPTHS * PLANE
    after = lax.rem(place + 1, total)
    before = lax.rem(place + total - 1, total)

    def of_place(at, at_head):
        return (lax.div(at, PLANE), lax.div(lax.rem(at, PLANE), 2), lax.rem(at, 2), at_head)

    def in_plane(q):
        return (z, lax.div(q, 2), lax.rem(q, 2), head)

    def in_depth(k):
        return (k, x, c, head)

    def in_head(k):
        return (z, x, c, k)

    def put(src, dst, ssem, rsem, device):
        return pltpu.make_async_remote_copy(
            src_ref=src, dst_ref=dst, send_sem=ssem, recv_sem=rsem, device_id=device, device_id_type=MESH
        )

    def others(me, count, act):
        def one(i, carry):
            act(lax.rem(me + i, count))
            return carry

        lax.fori_loop(1, count, one, 0)

    def all_of(ref, count, which):
        whole = ref.at[pl.ds(0, count)]
        return put(whole, whole, send_sem.at[which], recv_sem.at[which], in_head(lax.rem(head + 1, PEERS)))

    small = [
        (states, xs.at[pl.ds(HALO, ROWS), :]),
        (w_step, wt_in),
        (done, dn),
        (rewards, rw),
        (w_state, ws),
        (taps_st, tst),
        (taps_in, tin),
        (gain, gn),
        (weight, vw),
        (horizon, hz),
    ]
    local = [pltpu.make_async_copy(src, dst, local_sem.at[i]) for i, (src, dst) in enumerate(small)]

    def tile_copy(src, dst, slot, which):
        columns = pl.ds(pl.multiple_of(which * WIDE, WIDE), WIDE)
        return pltpu.make_async_copy(src.at[:, columns], dst.at[which], tile_sem.at[slot, which])

    def turned(j):
        return lax.rem(j + x, TILES)

    for copy in local:
        copy.start()
    for j in range(TILES):
        tile_copy(w_in, wi, 0, turned(j)).start()
    for j in range(TILES):
        tile_copy(w_gate, wg, 1, j).start()

    barrier = pltpu.get_barrier_semaphore()

    def greet(device):
        pl.semaphore_signal(barrier, inc=1, device_id=device, device_id_type=MESH)

    others(z, DEPTHS, lambda k: greet(in_depth(k)))
    greet(of_place(before, head))
    for k in range(PEERS):
        greet(of_place(after, k))
    others(here, PLANE, lambda q: greet(in_plane(q)))
    others(head, PEERS, lambda k: greet(in_head(k)))

    local[2].wait()
    local[3].wait()
    alive = 1.0 - dn[...].astype(F32)
    ext[...] = jnp.zeros((8, ROWS + LANES), F32)
    ext[0:1, 0:ROWS] = rw[...]
    ext[1:2, 0:ROWS] = alive
    part[...] = jnp.zeros((8, ROWS), F32)
    local[1].wait()
    wt[...] = jnp.concatenate(
        [wt_in[...].astype(F32), jnp.zeros((LANES - HEADS, DEPTH), F32)], axis=0
    ).astype(BF16)
    local[0].wait()

    pl.semaphore_wait(barrier, (PLANE - 1) + (DEPTHS - 1) + (PEERS - 1) + 1 + PEERS)

    halo = put(
        states.at[pl.ds(ROWS - HALO, HALO), :],
        xs.at[pl.ds(0, HALO), :],
        near_sem.at[0],
        near_sem.at[1],
        of_place(after, head),
    )
    halo.start()
    rim = put(
        ext.at[:, pl.ds(0, LANES)], recvr, near_sem.at[2], near_sem.at[3], of_place(before, head)
    )
    rim.start()

    step_pre = lax.dot_general(
        xs[HALO : HALO + ROWS, :],
        wt[...],
        (((1,), (1,)), ((), ())),
        preferred_element_type=F32,
    ).T[0:HEADS, :]
    order = lax.broadcasted_iota(jnp.int32, (HEADS, ROWS), 0)
    bias_rows = jnp.zeros((HEADS, ROWS), F32)
    rate_rows = jnp.zeros((HEADS, ROWS), F32)
    for h in range(HEADS):
        bias_rows = jnp.where(order == h, bias[h], bias_rows)
        rate_rows = jnp.where(order == h, rate[h], rate_rows)
    step_pre = step_pre + bias_rows
    step = jnp.maximum(step_pre, 0.0) + jnp.log1p(jnp.exp(-jnp.abs(step_pre)))
    dtrow[...] = step
    done_rows = jnp.broadcast_to(dn[...].astype(F32), (HEADS, ROWS))
    blocks = ROWS // LANES
    pieces = three_pieces(-(rate_rows * step)) + (done_rows,)
    stacked = jnp.concatenate(
        [p[:, b * LANES : (b + 1) * LANES] for p in pieces for b in range(blocks)], axis=0
    ).astype(BF16)
    triangle = (
        lax.broadcasted_iota(jnp.int32, (LANES, LANES), 0)
        <= lax.broadcasted_iota(jnp.int32, (LANES, LANES), 1)
    ).astype(F32).astype(BF16)
    sums = dot(stacked, triangle)
    span = HEADS * blocks
    decays = sums[0:span] + sums[span : 2 * span] + sums[2 * span : 3 * span]
    dones = sums[3 * span : 4 * span]

    def joined(parts):
        found, offset = [], jnp.zeros((HEADS, 1), F32)
        for b in range(blocks):
            block = parts[b * HEADS : (b + 1) * HEADS, :] + offset
            offset = block[:, LANES - 1 : LANES]
            found.append(block)
        return jnp.concatenate(found, axis=1), offset

    running, last = joined(decays)
    done_to, done_all = joined(dones)
    done_before = done_to - done_rows
    lrow[...] = running
    drow[...] = done_before
    tail[...] = jnp.where(done_before == done_all, jnp.exp(last - running) * step, 0.0)
    lost = jnp.broadcast_to(jnp.where(done_all == 0.0, jnp.exp(last), 0.0), (HEADS, LANES))
    decb[...] = lost
    others(
        here,
        PLANE,
        lambda q: put(decb, recve1.at[here], send_sem.at[0], recv_sem.at[0], in_plane(q)).start(),
    )
    recve1[here] = lost

    def convolved(pre, taps):
        whole = pre[HALO : HALO + HALF, :] * taps[KCONV - 1 : KCONV, :]
        for k in range(KCONV - 1):
            lag = KCONV - 1 - k
            whole = whole + pre[HALO - lag : HALO - lag + HALF, :] * taps[k : k + 1, :]
        return silu(whole)

    def project(pre, half, tile):
        rows = xs[half * HALF : half * HALF + HALO + HALF, :]
        pre[...] = dot(rows, ws[...] if tile is None else wi[tile])

    def finish(pre, half, tile):
        rows = slice(half * HALF, (half + 1) * HALF)
        if tile is None:
            conv = convolved(pre, tst[...])
            wtf[:, rows] = conv[:, 0:LANES].T
            ro[rows, :] = conv[:, LANES:WIDE]
            return
        taps = tin[:, pl.ds(pl.multiple_of(tile * WIDE, WIDE), WIDE)]
        conv = convolved(pre, taps).astype(BF16)
        for k in range(2):
            xh[tile * 2 + k, rows, :] = conv[:, k * LANES : (k + 1) * LANES]

    def gained(tile):
        for k in range(2):
            h = tile * 2 + k
            added = dot((wtf[...] * tail[pl.ds(h, 1), :]).astype(BF16), xh[h])
            send1[h] = added.astype(BF16)

    def send_gained(tile):
        for k in range(2):
            h = tile * 2 + k

            @pl.when(h != here)
            def _():
                put(
                    send1.at[h], recv1.at[here], send_sem.at[1], recv_sem.at[1], in_plane(h)
                ).start()

    def gate_tile(j):
        tile_copy(w_gate, wg, 1, j).wait()
        gate = silu(dot(xs[HALO : HALO + ROWS, :], wg[j]))
        for k in range(2):
            gs[j * 2 + k] = gate[:, k * LANES : (k + 1) * LANES]

    pres = (pre0, pre1)
    tiles = [None] + [turned(j) for j in range(TILES)]

    local[4].wait()
    local[5].wait()
    local[6].wait()
    project(pres[0], 1, None)
    for i in range(1, TILES + 1):
        tile_copy(w_in, wi, 0, tiles[i]).wait()
        project(pres[i % 2], 1, tiles[i])
        finish(pres[(i - 1) % 2], 1, tiles[i - 1])
    finish(pres[TILES % 2], 1, tiles[TILES])

    for j in range(EARLY):
        gate_tile(j)

    halo.wait_recv()
    xs[0:HALO, :] = jnp.where(place > 0, xs[0:HALO, :].astype(F32), 0.0).astype(BF16)
    project(pres[0], 0, None)
    for i in range(1, TILES + 1):
        project(pres[i % 2], 0, tiles[i])
        finish(pres[(i - 1) % 2], 0, tiles[i - 1])
        if i > 1:
            gained(tiles[i - 1])
            send_gained(tiles[i - 1])
    finish(pres[TILES % 2], 0, tiles[TILES])
    gained(tiles[TILES])
    send_gained(tiles[TILES])

    all_of(recve1, PLANE - 1, 0).wait_recv()
    plane_lost = recve1[0]
    for q in range(1, PLANE):
        plane_lost = plane_lost * recve1[q]
    dall[...] = plane_lost
    others(
        z,
        DEPTHS,
        lambda k: put(dall, recve2.at[z], send_sem.at[2], recv_sem.at[2], in_depth(k)).start(),
    )
    recve2[z] = plane_lost
    recv1[here] = send1[here]

    for j in range(EARLY, TILES):
        gate_tile(j)

    all_of(recv1, PLANE - 1, 1).wait_recv()

    def plane_step(q, carry):
        state, lasting = carry
        inside[q] = state
        reach_in[q] = jnp.broadcast_to(lasting, (8, LANES))
        lost = recve1[q, pl.ds(here, 1), :]
        return lost * state + recv1[q].astype(F32), lasting * lost

    state, _ = lax.fori_loop(
        0, PLANE, plane_step, (jnp.zeros((LANES, LANES), F32), jnp.ones((1, LANES), F32))
    )
    send2[...] = state.astype(BF16)

    def to_later(k):
        return put(send2, recv2.at[z], s2.at[k], r2.at[z], in_depth(k))

    def later(act):
        def one(k, carry):
            act(k)
            return carry

        lax.fori_loop(z + 1, DEPTHS, one, 0)

    later(lambda k: to_later(k).start())

    done_row = drow[0:1, :]
    done_down = down(done_row)
    rdm[...] = jnp.where(done_down == 0.0, ro[...], 0.0)
    readout = ro[...].astype(BF16)
    writes_t = wtf[...].astype(BF16)
    for b in range(2):
        rows = slice(b * WIDE, (b + 1) * WIDE)
        upto = (b + 1) * WIDE
        scores = dot(readout[rows, :], writes_t[:, 0:upto])
        at_row = lax.broadcasted_iota(jnp.int32, (WIDE, LANES), 0) + b * WIDE
        for k in range(upto // LANES):
            columns = slice(k * LANES, (k + 1) * LANES)
            at_column = lax.broadcasted_iota(jnp.int32, (WIDE, LANES), 1) + k * LANES
            seen = (at_row >= at_column) & (done_down[rows, :] == done_row[:, columns])
            sc[rows, columns] = jnp.where(seen, scores[:, columns], 0.0)

    def own_scan(h, carry):
        across = lrow[pl.ds(h, 1), :]
        step_across = dtrow[pl.ds(h, 1), :]
        along = down(across)
        inner = xh[h]
        for b in range(2):
            rows = slice(b * WIDE, (b + 1) * WIDE)
            upto = (b + 1) * WIDE
            weights = []
            for k in range(upto // LANES):
                columns = slice(k * LANES, (k + 1) * LANES)
                gap = jnp.minimum(along[rows, :] - across[:, columns], 0.0)
                weights.append((jnp.exp(gap) * step_across[:, columns] * sc[rows, columns]).astype(BF16))
            mixed = dot(jnp.concatenate(weights, axis=1), inner[0:upto, :])
            y[h, rows, :] = mixed + skip[h] * inner[rows, :].astype(F32)
        rs[h] = (rdm[...] * jnp.exp(along)).astype(BF16)
        return carry

    lax.fori_loop(0, HEADS - 2, own_scan, 0)

    all_of(recve2, DEPTHS - 1, 2).wait_recv()

    def depth_step(k, state):
        put(send2, recv2.at[k], s2.at[k], r2.at[k], in_depth(k)).wait_recv()
        return recve2[k, pl.ds(here, 1), :] * state + recv2[k].astype(F32)

    entering = lax.fori_loop(0, z, depth_step, jnp.zeros((LANES, LANES), F32))

    def carried(q):
        send4[q] = (reach_in[q][0:1, :] * entering + inside[q]).astype(BF16)

    def hand_out(q):
        carried(q)
        put(send4.at[q], recv4.at[here], send_sem.at[3], recv_sem.at[3], in_plane(q)).start()

    others(here, PLANE, hand_out)
    carried(here)
    recv4[here] = send4[here]

    lax.fori_loop(HEADS - 2, HEADS, own_scan, 0)

    local[7].wait()
    local[8].wait()
    local[9].wait()
    rim.wait_recv()
    is_last = place == total - 1
    ext[:, ROWS : ROWS + LANES] = jnp.where(is_last, 0.0, recvr[...])
    length = ROWS + LANES
    survive = jnp.ones((1, ROWS), F32)
    rewarded = jnp.zeros((1, ROWS), F32)
    for k in range(NSTEP + 1):
        ahead = ext[...] if k == 0 else pltpu.roll(ext[...], length - k, 1)
        factor = DISCOUNT**k * survive
        rewarded = rewarded + jnp.where(k < hz[...], factor * ahead[0:1, 0:ROWS], 0.0)
        coef[k : k + 1, :] = jnp.where(k == hz[...], factor, 0.0)
        survive = survive * ahead[1:2, 0:ROWS]
    coef[NSTEP + 1 : NSTEP + 2, :] = rewarded
    gn[...] = gn[...] * vw[...]

    all_of(recv4, PLANE - 1, 3).wait_recv()

    def mix(b, carry):
        rows = pl.ds(pl.multiple_of(b * LANES, LANES), LANES)
        squares = jnp.zeros((LANES, LANES), F32)
        valued = jnp.zeros((LANES, LANES), F32)
        for h in range(HEADS):
            mixed = y[h, rows, :] + dot(rs[h, rows, :], recv4[h])
            gated = mixed * gs[h, rows, :]
            squares = squares + gated * gated
            valued = valued + gated * gn[:, h * LANES : (h + 1) * LANES]
        part[0:1, rows] = jnp.sum(squares.T, axis=0, keepdims=True)
        part[1:2, rows] = jnp.sum(valued.T, axis=0, keepdims=True)
        return carry

    lax.fori_loop(0, ROWS // LANES, mix, 0)

    def to_before(k):
        return put(
            part.at[:, pl.ds(0, LANES)],
            recvn.at[head],
            send_sem.at[5],
            recv_sem.at[5],
            of_place(before, k),
        )

    for k in range(PEERS):
        to_before(k).start()
    others(
        head,
        PEERS,
        lambda k: put(part, recvh.at[head], send_sem.at[4], recv_sem.at[4], in_head(k)).start(),
    )
    recvh[head] = part[...]
    all_of(recvh, PEERS - 1, 4).wait_recv()
    all_of(recvn, PEERS, 5).wait_recv()

    def normed(sums):
        return sums[1:2, :] * lax.rsqrt(sums[0:1, :] / (PEERS * HEADS * LANES) + EPSILON)

    own = normed(recvh[0] + recvh[1] + recvh[2] + recvh[3])
    following = normed(recvn[0] + recvn[1] + recvn[2] + recvn[3])
    following = jnp.where(is_last, 0.0, following)
    valued = jnp.broadcast_to(jnp.concatenate([own, following], axis=1), (8, length))
    targets = coef[NSTEP + 1 : NSTEP + 2, :]
    for k in range(NSTEP + 1):
        ahead = valued if k == 0 else pltpu.roll(valued, length - k, 1)
        targets = targets + coef[k : k + 1, :] * ahead[0:1, 0:ROWS]
    residual = targets - own
    terms = jnp.where(residual < 0, 1.0 - EXPECTILE, EXPECTILE) * residual * residual
    mine = jnp.broadcast_to(jnp.sum(terms, axis=1, keepdims=True), (1, LANES))
    loss1[...] = mine

    def tell(device):
        put(loss1, recvl.at[place], send_sem.at[6], recv_sem.at[6], device).start()

    def tell_plane(k):
        for q in range(PLANE):
            tell((k, q // 2, q % 2, head))

    others(z, DEPTHS, tell_plane)
    others(here, PLANE, lambda q: tell(in_plane(q)))
    recvl[place] = mine
    out[0:1, :] = own
    out[1:2, :] = targets

    halo.wait_send()
    rim.wait_send()
    all_of(recve1, PLANE - 1, 0).wait_send()
    all_of(recv1, PLANE - 1, 1).wait_send()
    all_of(recve2, DEPTHS - 1, 2).wait_send()
    all_of(recv4, PLANE - 1, 3).wait_send()
    all_of(recvh, PEERS - 1, 4).wait_send()
    all_of(recvn, PEERS, 5).wait_send()
    later(lambda k: to_later(k).wait_send())

    all_of(recvl, total - 1, 6).wait_recv()
    summed = jnp.sum(recvl[...], axis=0) / seq_total
    out[2:8, :] = jnp.broadcast_to(summed[:, 0:1], (6, ROWS))
    all_of(recvl, total - 1, 6).wait_send()


def scratch():
    v = pltpu.VMEM
    dma = pltpu.SemaphoreType.DMA
    return [
        v((HALO + ROWS, DEPTH), BF16),
        v((TILES, DEPTH, WIDE), BF16),
        v((TILES, DEPTH, WIDE), BF16),
        v((DEPTH, WIDE), BF16),
        v((HEADS, DEPTH), BF16),
        v((LANES, DEPTH), BF16),
        v((KCONV, HEADS * LANES), F32),
        v((KCONV, WIDE), F32),
        v((1, HEADS * LANES), F32),
        v((1, HEADS * LANES), F32),
        v((1, ROWS), F32),
        v((1, ROWS), jnp.int32),
        v((1, ROWS), jnp.int32),
        v((HALO + HALF, WIDE), F32),
        v((HALO + HALF, WIDE), F32),
        v((HEADS, ROWS, LANES), BF16),
        v((ROWS, LANES), F32),
        v((ROWS, LANES), F32),
        v((LANES, ROWS), F32),
        v((ROWS, ROWS), F32),
        v((HEADS, ROWS), F32),
        v((HEADS, ROWS), F32),
        v((HEADS, ROWS), F32),
        v((HEADS, ROWS), F32),
        v((HEADS, LANES), F32),
        v((PLANE, HEADS, LANES), F32),
        v((HEADS, LANES), F32),
        v((DEPTHS, HEADS, LANES), F32),
        v((HEADS, ROWS, LANES), F32),
        v((HEADS, ROWS, LANES), F32),
        v((HEADS, ROWS, LANES), BF16),
        v((PLANE, LANES, LANES), BF16),
        v((PLANE, LANES, LANES), BF16),
        v((PLANE, LANES, LANES), F32),
        v((PLANE, 8, LANES), F32),
        v((LANES, LANES), BF16),
        v((DEPTHS, LANES, LANES), BF16),
        v((PLANE, LANES, LANES), BF16),
        v((PLANE, LANES, LANES), BF16),
        v((8, ROWS), F32),
        v((PEERS, 8, ROWS), F32),
        v((PEERS, 8, LANES), F32),
        v((8, ROWS + LANES), F32),
        v((8, LANES), F32),
        v((16, ROWS), F32),
        v((1, LANES), F32),
        v((DEPTHS * PLANE, 1, LANES), F32),
        dma((10,)),
        dma((2, TILES)),
        dma((4,)),
        dma((7,)),
        dma((7,)),
        dma((DEPTHS,)),
        dma((DEPTHS,)),
    ]


def per_device(
    states,
    inner_weight,
    gate_weight,
    state_weight,
    step_weight,
    step_bias,
    decay_rate,
    skip_gain,
    conv_inner,
    conv_state,
    norm_gain,
    value_weight,
    rewards,
    done_flags,
    horizon,
):
    hbm = pl.BlockSpec(memory_space=pl.ANY)
    smem = pl.BlockSpec(memory_space=pltpu.SMEM)
    vmem = pl.BlockSpec(memory_space=pltpu.VMEM)
    seq_total = states.shape[0] * DEPTHS * PLANE
    packed = pl.pallas_call(
        functools.partial(kernel, seq_total),
        out_shape=jax.ShapeDtypeStruct((8, ROWS), F32),
        in_specs=[hbm] * 5 + [smem] * 3 + [hbm] * 7,
        out_specs=vmem,
        scratch_shapes=scratch(),
        compiler_params=pltpu.CompilerParams(
            collective_id=0, has_side_effects=True, vmem_limit_bytes=56 * 2**20
        ),
    )(
        states,
        inner_weight,
        gate_weight,
        state_weight,
        step_weight.T,
        step_bias,
        decay_rate,
        skip_gain,
        conv_inner,
        conv_state,
        norm_gain.reshape(1, -1),
        value_weight.reshape(1, -1),
        rewards.reshape(1, -1),
        done_flags.reshape(1, -1),
        horizon.reshape(1, -1),
    )
    return packed[0], packed[1], packed[2, 0]


def solution(mesh):
    torus = Mesh(
        mesh.devices.reshape(DEPTHS, 4, 2, mesh.shape["head"]), SEQ + ("head",)
    )
    placed = (
        P(SEQ, None),
        P(None, "head"),
        P(None, "head"),
        P(),
        P(None, "head"),
        P("head"),
        P("head"),
        P("head"),
        P(None, "head"),
        P(),
        P("head"),
        P("head"),
        P(SEQ),
        P(SEQ),
        P(SEQ),
    )
    return jax.shard_map(
        per_device, mesh=torus, in_specs=placed, out_specs=(P(SEQ), P(SEQ), P()), check_vma=False
    )
```

```python
import functools

import jax
import jax.numpy as jnp
from jax import lax
from jax.experimental import pallas as pl
from jax.experimental.pallas import tpu as pltpu
from jax.sharding import Mesh
from jax.sharding import PartitionSpec as P

SEQ = ("seq_0", "seq_1", "seq_2")
MESH = pl.DeviceIdType.MESH
F32 = jnp.float32
BF16 = jnp.bfloat16

KCONV = 4
NSTEP = 8
DISCOUNT = 0.99
EXPECTILE = 0.7
EPSILON = 1e-05

HALO = 16
ROWS = 512
HALF = 256
EARLY = 0
DEPTH = 2048
HEADS = 8
LANES = 128
WIDE = 256
TILE = 512
TILES = HEADS * LANES // TILE
TILE_HEADS = TILE // LANES
PLANE = 8
DEPTHS = 8
PEERS = 4


def silu(value):
    half = 0.5 * value
    return half + half * jnp.tanh(half)


def dot(a, b):
    return jnp.dot(a, b, preferred_element_type=F32)


def three_pieces(value):
    high = value.astype(BF16).astype(F32)
    rest = value - high
    middle = rest.astype(BF16).astype(F32)
    return high, middle, rest - middle


def down(row, rows=LANES):
    return jnp.broadcast_to(row, (rows, row.shape[1])).T


def kernel(
    seq_total,
    states,
    w_in,
    w_gate,
    w_state,
    w_step,
    bias_in,
    rate_in,
    skip_in,
    taps_in,
    taps_st,
    gain,
    weight,
    rewards,
    done,
    horizon,
    out,
    xs,
    wi,
    wg,
    ws,
    wt_in,
    bias,
    rate,
    skip,
    wt,
    tin,
    tst,
    gn,
    vw,
    rw,
    dn,
    hz,
    pre0,
    pre1,
    xh,
    ro,
    rdm,
    wtf,
    sc,
    lrow,
    dtrow,
    drow,
    tail,
    decb,
    recve1,
    dall,
    recve2,
    y,
    gs,
    send1,
    recv1,
    inside,
    reach_in,
    send2,
    recv2,
    send4,
    recv4,
    part,
    recvh,
    recvn,
    ext,
    recvr,
    coef,
    loss1,
    recvl,
    local_sem,
    tile_sem,
    near_sem,
    send_sem,
    recv_sem,
    s2,
    r2,
):
    z, x, c, head = (lax.axis_index(name) for name in SEQ + ("head",))
    here = x * 2 + c
    place = z * PLANE + here
    total = DEPTHS * PLANE
    after = lax.rem(place + 1, total)
    before = lax.rem(place + total - 1, total)

    def of_place(at, at_head):
        return (lax.div(at, PLANE), lax.div(lax.rem(at, PLANE), 2), lax.rem(at, 2), at_head)

    def in_plane(q):
        return (z, lax.div(q, 2), lax.rem(q, 2), head)

    def in_depth(k):
        return (k, x, c, head)

    def in_head(k):
        return (z, x, c, k)

    def put(src, dst, ssem, rsem, device):
        return pltpu.make_async_remote_copy(
            src_ref=src, dst_ref=dst, send_sem=ssem, recv_sem=rsem, device_id=device, device_id_type=MESH
        )

    def others(me, count, act):
        def one(i, carry):
            act(lax.rem(me + i, count))
            return carry

        lax.fori_loop(1, count, one, 0)

    def all_of(ref, count, which):
        whole = ref.at[pl.ds(0, count)]
        return put(whole, whole, send_sem.at[which], recv_sem.at[which], in_head(lax.rem(head + 1, PEERS)))

    small = [
        (states, xs.at[pl.ds(HALO, ROWS), :]),
        (w_step, wt_in),
        (bias_in, bias),
        (rate_in, rate),
        (skip_in, skip),
        (done, dn),
        (rewards, rw),
        (w_state, ws),
        (taps_st, tst),
        (taps_in, tin),
        (gain, gn),
        (weight, vw),
        (horizon, hz),
    ]
    local = [pltpu.make_async_copy(src, dst, local_sem.at[i]) for i, (src, dst) in enumerate(small)]

    def tile_copy(src, dst, slot, which):
        columns = pl.ds(pl.multiple_of(which * TILE, TILE), TILE)
        return pltpu.make_async_copy(src.at[:, columns], dst.at[which], tile_sem.at[slot, which])

    def turned(j):
        return lax.rem(j + x, TILES)

    for copy in local:
        copy.start()
    for j in range(TILES):
        tile_copy(w_in, wi, 0, turned(j)).start()

    barrier = pltpu.get_barrier_semaphore()

    def greet(device):
        pl.semaphore_signal(barrier, inc=1, device_id=device, device_id_type=MESH)

    others(z, DEPTHS, lambda k: greet(in_depth(k)))
    greet(of_place(before, head))
    for k in range(PEERS):
        greet(of_place(after, k))
    others(here, PLANE, lambda q: greet(in_plane(q)))
    others(head, PEERS, lambda k: greet(in_head(k)))

    local[5].wait()
    local[6].wait()
    alive = 1.0 - dn[...].astype(F32)
    ext[...] = jnp.zeros((8, ROWS + LANES), F32)
    ext[0:1, 0:ROWS] = rw[...]
    ext[1:2, 0:ROWS] = alive
    part[...] = jnp.zeros((8, ROWS), F32)
    local[1].wait()
    wt[...] = jnp.concatenate(
        [wt_in[...].astype(F32), jnp.zeros((LANES - HEADS, DEPTH), F32)], axis=0
    ).astype(BF16)
    local[0].wait()

    pl.semaphore_wait(barrier, (PLANE - 1) + (DEPTHS - 1) + (PEERS - 1) + 1 + PEERS)

    halo = put(
        states.at[pl.ds(ROWS - HALO, HALO), :],
        xs.at[pl.ds(0, HALO), :],
        near_sem.at[0],
        near_sem.at[1],
        of_place(after, head),
    )
    halo.start()
    rim = put(
        ext.at[:, pl.ds(0, LANES)], recvr, near_sem.at[2], near_sem.at[3], of_place(before, head)
    )
    rim.start()

    step_pre = lax.dot_general(
        xs[HALO : HALO + ROWS, :],
        wt[...],
        (((1,), (1,)), ((), ())),
        preferred_element_type=F32,
    ).T[0:HEADS, :]
    for i in (2, 3, 4):
        local[i].wait()
    order = lax.broadcasted_iota(jnp.int32, (HEADS, ROWS), 0)
    bias_rows = jnp.zeros((HEADS, ROWS), F32)
    rate_rows = jnp.zeros((HEADS, ROWS), F32)
    for h in range(HEADS):
        bias_rows = jnp.where(order == h, bias[h], bias_rows)
        rate_rows = jnp.where(order == h, rate[h], rate_rows)
    step_pre = step_pre + bias_rows
    step = jnp.maximum(step_pre, 0.0) + jnp.log1p(jnp.exp(-jnp.abs(step_pre)))
    dtrow[...] = step
    done_rows = jnp.broadcast_to(dn[...].astype(F32), (HEADS, ROWS))
    blocks = ROWS // LANES
    pieces = three_pieces(-(rate_rows * step)) + (done_rows,)
    stacked = jnp.concatenate(
        [p[:, b * LANES : (b + 1) * LANES] for p in pieces for b in range(blocks)], axis=0
    ).astype(BF16)
    triangle = (
        lax.broadcasted_iota(jnp.int32, (LANES, LANES), 0)
        <= lax.broadcasted_iota(jnp.int32, (LANES, LANES), 1)
    ).astype(F32).astype(BF16)
    sums = dot(stacked, triangle)
    span = HEADS * blocks
    decays = sums[0:span] + sums[span : 2 * span] + sums[2 * span : 3 * span]
    dones = sums[3 * span : 4 * span]

    def joined(parts):
        found, offset = [], jnp.zeros((HEADS, 1), F32)
        for b in range(blocks):
            block = parts[b * HEADS : (b + 1) * HEADS, :] + offset
            offset = block[:, LANES - 1 : LANES]
            found.append(block)
        return jnp.concatenate(found, axis=1), offset

    running, last = joined(decays)
    done_to, done_all = joined(dones)
    done_before = done_to - done_rows
    lrow[...] = running
    drow[...] = done_before
    tail[...] = jnp.where(done_before == done_all, jnp.exp(last - running) * step, 0.0)
    lost = jnp.broadcast_to(jnp.where(done_all == 0.0, jnp.exp(last), 0.0), (HEADS, LANES))
    decb[...] = lost
    others(
        here,
        PLANE,
        lambda q: put(decb, recve1.at[here], send_sem.at[0], recv_sem.at[0], in_plane(q)).start(),
    )
    recve1[here] = lost

    def convolved(pre, taps, columns):
        whole = pre[HALO : HALO + HALF, columns] * taps[KCONV - 1 : KCONV, :]
        for k in range(KCONV - 1):
            lag = KCONV - 1 - k
            whole = whole + pre[HALO - lag : HALO - lag + HALF, columns] * taps[k : k + 1, :]
        return silu(whole)

    def project(pre, half, tile):
        rows = xs[half * HALF : half * HALF + HALO + HALF, :]
        if tile is None:
            pre[:, 0:WIDE] = dot(rows, ws[...])
        else:
            pre[...] = dot(rows, wi[tile])

    def finish(pre, half, tile):
        rows = slice(half * HALF, (half + 1) * HALF)
        if tile is None:
            wtf[:, rows] = convolved(pre, tst[:, 0:LANES], slice(0, LANES)).T
            ro[rows, :] = convolved(pre, tst[:, LANES:WIDE], slice(LANES, WIDE))
            return
        for k in range(TILE_HEADS):
            h = tile * TILE_HEADS + k
            taps = tin[:, pl.ds(pl.multiple_of(h * LANES, LANES), LANES)]
            conv = convolved(pre, taps, slice(k * LANES, (k + 1) * LANES))
            xh[h, rows, :] = conv.astype(BF16)

    def gained(tile):
        for k in range(TILE_HEADS):
            h = tile * TILE_HEADS + k
            added = dot((wtf[...] * tail[pl.ds(h, 1), :]).astype(BF16), xh[h])
            send1[h] = added.astype(BF16)

    def send_gained(tile):
        for k in range(TILE_HEADS):
            h = tile * TILE_HEADS + k

            @pl.when(h != here)
            def _():
                put(
                    send1.at[h], recv1.at[here], send_sem.at[1], recv_sem.at[1], in_plane(h)
                ).start()

    def gate_tile(j):
        tile_copy(w_gate, wg, 1, j).wait()
        gate = silu(dot(xs[HALO : HALO + ROWS, :], wg[j]))
        for k in range(TILE_HEADS):
            gs[j * TILE_HEADS + k] = gate[:, k * LANES : (k + 1) * LANES]

    pres = (pre0, pre1)
    tiles = [None] + [turned(j) for j in range(TILES)]

    for i in (7, 8, 9):
        local[i].wait()
    project(pres[0], 1, None)
    for i in range(1, TILES + 1):
        tile_copy(w_in, wi, 0, tiles[i]).wait()
        project(pres[i % 2], 1, tiles[i])
        finish(pres[(i - 1) % 2], 1, tiles[i - 1])
    for j in range(TILES):
        tile_copy(w_gate, wg, 1, j).start()
    finish(pres[TILES % 2], 1, tiles[TILES])

    for j in range(EARLY):
        gate_tile(j)

    halo.wait_recv()
    xs[0:HALO, :] = jnp.where(place > 0, xs[0:HALO, :].astype(F32), 0.0).astype(BF16)
    project(pres[0], 0, None)
    for i in range(1, TILES + 1):
        project(pres[i % 2], 0, tiles[i])
        finish(pres[(i - 1) % 2], 0, tiles[i - 1])
        if i > 1:
            gained(tiles[i - 1])
            send_gained(tiles[i - 1])
    finish(pres[TILES % 2], 0, tiles[TILES])
    gained(tiles[TILES])
    send_gained(tiles[TILES])

    all_of(recve1, PLANE - 1, 0).wait_recv()
    plane_lost = recve1[0]
    for q in range(1, PLANE):
        plane_lost = plane_lost * recve1[q]
    dall[...] = plane_lost
    others(
        z,
        DEPTHS,
        lambda k: put(dall, recve2.at[z], send_sem.at[2], recv_sem.at[2], in_depth(k)).start(),
    )
    recve2[z] = plane_lost
    recv1[here] = send1[here]

    for j in range(EARLY, TILES):
        gate_tile(j)

    all_of(recv1, PLANE - 1, 1).wait_recv()

    def plane_step(q, carry):
        state, lasting = carry
        inside[q] = state
        reach_in[q] = jnp.broadcast_to(lasting, (8, LANES))
        lost = recve1[q, pl.ds(here, 1), :]
        return lost * state + recv1[q].astype(F32), lasting * lost

    state, _ = lax.fori_loop(
        0, PLANE, plane_step, (jnp.zeros((LANES, LANES), F32), jnp.ones((1, LANES), F32))
    )
    send2[...] = state.astype(BF16)

    def to_later(k):
        return put(send2, recv2.at[z], s2.at[k], r2.at[z], in_depth(k))

    def later(act):
        def one(k, carry):
            act(k)
            return carry

        lax.fori_loop(z + 1, DEPTHS, one, 0)

    later(lambda k: to_later(k).start())

    done_row = drow[0:1, :]
    done_down = down(done_row)
    rdm[...] = jnp.where(done_down == 0.0, ro[...], 0.0).astype(BF16)
    readout = ro[...].astype(BF16)
    writes_t = wtf[...].astype(BF16)
    for b in range(2):
        rows = slice(b * WIDE, (b + 1) * WIDE)
        upto = (b + 1) * WIDE
        scores = dot(readout[rows, :], writes_t[:, 0:upto])
        at_row = lax.broadcasted_iota(jnp.int32, (WIDE, LANES), 0) + b * WIDE
        for k in range(upto // LANES):
            columns = slice(k * LANES, (k + 1) * LANES)
            at_column = lax.broadcasted_iota(jnp.int32, (WIDE, LANES), 1) + k * LANES
            seen = (at_row >= at_column) & (done_down[rows, :] == done_row[:, columns])
            sc[rows, columns] = jnp.where(seen, scores[:, columns], 0.0)

    def own_scan(h, carry):
        across = lrow[pl.ds(h, 1), :]
        step_across = dtrow[pl.ds(h, 1), :]
        along = down(across)
        inner = xh[h]
        for b in range(2):
            rows = slice(b * WIDE, (b + 1) * WIDE)
            upto = (b + 1) * WIDE
            weights = []
            for k in range(upto // LANES):
                columns = slice(k * LANES, (k + 1) * LANES)
                gap = jnp.minimum(along[rows, :] - across[:, columns], 0.0)
                weights.append((jnp.exp(gap) * step_across[:, columns] * sc[rows, columns]).astype(BF16))
            mixed = dot(jnp.concatenate(weights, axis=1), inner[0:upto, :])
            y[h, rows, :] = (mixed + skip[h] * inner[rows, :].astype(F32)) * gs[h, rows, :]
        gs[h] = jnp.exp(along) * gs[h]
        return carry

    lax.fori_loop(0, HEADS - 2, own_scan, 0)

    all_of(recve2, DEPTHS - 1, 2).wait_recv()

    def depth_step(k, state):
        put(send2, recv2.at[k], s2.at[k], r2.at[k], in_depth(k)).wait_recv()
        return recve2[k, pl.ds(here, 1), :] * state + recv2[k].astype(F32)

    entering = lax.fori_loop(0, z, depth_step, jnp.zeros((LANES, LANES), F32))

    def carried(q):
        send4[q] = (reach_in[q][0:1, :] * entering + inside[q]).astype(BF16)

    def hand_out(q):
        carried(q)
        put(send4.at[q], recv4.at[here], send_sem.at[3], recv_sem.at[3], in_plane(q)).start()

    others(here, PLANE, hand_out)
    carried(here)
    recv4[here] = send4[here]

    lax.fori_loop(HEADS - 2, HEADS, own_scan, 0)

    for i in (10, 11, 12):
        local[i].wait()
    rim.wait_recv()
    is_last = place == total - 1
    ext[:, ROWS : ROWS + LANES] = jnp.where(is_last, 0.0, recvr[...])
    length = ROWS + LANES
    survive = jnp.ones((1, ROWS), F32)
    rewarded = jnp.zeros((1, ROWS), F32)
    for k in range(NSTEP + 1):
        ahead = ext[...] if k == 0 else pltpu.roll(ext[...], length - k, 1)
        factor = DISCOUNT**k * survive
        rewarded = rewarded + jnp.where(k < hz[...], factor * ahead[0:1, 0:ROWS], 0.0)
        coef[k : k + 1, :] = jnp.where(k == hz[...], factor, 0.0)
        survive = survive * ahead[1:2, 0:ROWS]
    coef[NSTEP + 1 : NSTEP + 2, :] = rewarded
    gn[...] = gn[...] * vw[...]

    all_of(recv4, PLANE - 1, 3).wait_recv()

    carried_in = jnp.concatenate([recv4[h] for h in range(HEADS)], axis=1)

    def mix(b, carry):
        rows = pl.ds(pl.multiple_of(b * LANES, LANES), LANES)
        reached = dot(rdm[rows, :], carried_in)
        squares = jnp.zeros((LANES, LANES), F32)
        valued = jnp.zeros((LANES, LANES), F32)
        for h in range(HEADS):
            columns = slice(h * LANES, (h + 1) * LANES)
            gated = y[h, rows, :] + reached[:, columns] * gs[h, rows, :]
            squares = squares + gated * gated
            valued = valued + gated * gn[:, columns]
        part[0:1, rows] = jnp.sum(squares.T, axis=0, keepdims=True)
        part[1:2, rows] = jnp.sum(valued.T, axis=0, keepdims=True)
        return carry

    lax.fori_loop(0, ROWS // LANES, mix, 0)

    def to_before(k):
        return put(
            part.at[:, pl.ds(0, LANES)],
            recvn.at[head],
            send_sem.at[5],
            recv_sem.at[5],
            of_place(before, k),
        )

    for k in range(PEERS):
        to_before(k).start()
    others(
        head,
        PEERS,
        lambda k: put(part, recvh.at[head], send_sem.at[4], recv_sem.at[4], in_head(k)).start(),
    )
    recvh[head] = part[...]
    all_of(recvh, PEERS - 1, 4).wait_recv()
    all_of(recvn, PEERS, 5).wait_recv()

    def normed(sums):
        return sums[1:2, :] * lax.rsqrt(sums[0:1, :] / (PEERS * HEADS * LANES) + EPSILON)

    own = normed(recvh[0] + recvh[1] + recvh[2] + recvh[3])
    following = normed(recvn[0] + recvn[1] + recvn[2] + recvn[3])
    following = jnp.where(is_last, 0.0, following)
    valued = jnp.broadcast_to(jnp.concatenate([own, following], axis=1), (8, length))
    targets = coef[NSTEP + 1 : NSTEP + 2, :]
    for k in range(NSTEP + 1):
        ahead = valued if k == 0 else pltpu.roll(valued, length - k, 1)
        targets = targets + coef[k : k + 1, :] * ahead[0:1, 0:ROWS]
    residual = targets - own
    terms = jnp.where(residual < 0, 1.0 - EXPECTILE, EXPECTILE) * residual * residual
    mine = jnp.broadcast_to(jnp.sum(terms, axis=1, keepdims=True), (1, LANES))
    loss1[...] = mine

    def tell(device):
        put(loss1, recvl.at[place], send_sem.at[6], recv_sem.at[6], device).start()

    def tell_plane(k):
        for q in range(PLANE):
            tell((k, q // 2, q % 2, head))

    others(z, DEPTHS, tell_plane)
    others(here, PLANE, lambda q: tell(in_plane(q)))
    recvl[place] = mine
    out[0:1, :] = own
    out[1:2, :] = targets

    halo.wait_send()
    rim.wait_send()
    all_of(recve1, PLANE - 1, 0).wait_send()
    all_of(recv1, PLANE - 1, 1).wait_send()
    all_of(recve2, DEPTHS - 1, 2).wait_send()
    all_of(recv4, PLANE - 1, 3).wait_send()
    all_of(recvh, PEERS - 1, 4).wait_send()
    all_of(recvn, PEERS, 5).wait_send()
    later(lambda k: to_later(k).wait_send())

    all_of(recvl, total - 1, 6).wait_recv()
    summed = jnp.sum(recvl[...], axis=0) / seq_total
    out[2:8, :] = jnp.broadcast_to(summed[:, 0:1], (6, ROWS))
    all_of(recvl, total - 1, 6).wait_send()


def unpack(packed, values, targets, loss):
    values[...] = packed[0:1, :]
    targets[...] = packed[1:2, :]
    loss[...] = packed[2:3, 0:1]


def scratch():
    v = pltpu.VMEM
    dma = pltpu.SemaphoreType.DMA
    return [
        v((HALO + ROWS, DEPTH), BF16),
        v((TILES, DEPTH, TILE), BF16),
        v((TILES, DEPTH, TILE), BF16),
        v((DEPTH, WIDE), BF16),
        v((HEADS, DEPTH), BF16),
        pltpu.SMEM((HEADS,), F32),
        pltpu.SMEM((HEADS,), F32),
        pltpu.SMEM((HEADS,), F32),
        v((LANES, DEPTH), BF16),
        v((KCONV, HEADS * LANES), F32),
        v((KCONV, WIDE), F32),
        v((1, HEADS * LANES), F32),
        v((1, HEADS * LANES), F32),
        v((1, ROWS), F32),
        v((1, ROWS), jnp.int32),
        v((1, ROWS), jnp.int32),
        v((HALO + HALF, TILE), F32),
        v((HALO + HALF, TILE), F32),
        v((HEADS, ROWS, LANES), BF16),
        v((ROWS, LANES), F32),
        v((ROWS, LANES), BF16),
        v((LANES, ROWS), F32),
        v((ROWS, ROWS), F32),
        v((HEADS, ROWS), F32),
        v((HEADS, ROWS), F32),
        v((HEADS, ROWS), F32),
        v((HEADS, ROWS), F32),
        v((HEADS, LANES), F32),
        v((PLANE, HEADS, LANES), F32),
        v((HEADS, LANES), F32),
        v((DEPTHS, HEADS, LANES), F32),
        v((HEADS, ROWS, LANES), F32),
        v((HEADS, ROWS, LANES), F32),
        v((PLANE, LANES, LANES), BF16),
        v((PLANE, LANES, LANES), BF16),
        v((PLANE, LANES, LANES), F32),
        v((PLANE, 8, LANES), F32),
        v((LANES, LANES), BF16),
        v((DEPTHS, LANES, LANES), BF16),
        v((PLANE, LANES, LANES), BF16),
        v((PLANE, LANES, LANES), BF16),
        v((8, ROWS), F32),
        v((PEERS, 8, ROWS), F32),
        v((PEERS, 8, LANES), F32),
        v((8, ROWS + LANES), F32),
        v((8, LANES), F32),
        v((16, ROWS), F32),
        v((1, LANES), F32),
        v((DEPTHS * PLANE, 1, LANES), F32),
        dma((13,)),
        dma((2, TILES)),
        dma((4,)),
        dma((7,)),
        dma((7,)),
        dma((DEPTHS,)),
        dma((DEPTHS,)),
    ]


def per_device(
    states,
    inner_weight,
    gate_weight,
    state_weight,
    step_weight,
    step_bias,
    decay_rate,
    skip_gain,
    conv_inner,
    conv_state,
    norm_gain,
    value_weight,
    rewards,
    done_flags,
    horizon,
):
    hbm = pl.BlockSpec(memory_space=pl.ANY)
    vmem = pl.BlockSpec(memory_space=pltpu.VMEM)
    seq_total = states.shape[0] * DEPTHS * PLANE
    packed = pl.pallas_call(
        functools.partial(kernel, seq_total),
        out_shape=jax.ShapeDtypeStruct((8, ROWS), F32),
        in_specs=[hbm] * 15,
        out_specs=vmem,
        scratch_shapes=scratch(),
        compiler_params=pltpu.CompilerParams(
            collective_id=0, has_side_effects=True, vmem_limit_bytes=56 * 2**20
        ),
    )(
        states,
        inner_weight,
        gate_weight,
        state_weight,
        step_weight.T,
        step_bias,
        decay_rate,
        skip_gain,
        conv_inner,
        conv_state,
        norm_gain.reshape(1, -1),
        value_weight.reshape(1, -1),
        rewards.reshape(1, -1),
        done_flags.reshape(1, -1),
        horizon.reshape(1, -1),
    )
    values, targets, loss = pl.pallas_call(
        unpack,
        out_shape=(
            jax.ShapeDtypeStruct((1, ROWS), F32),
            jax.ShapeDtypeStruct((1, ROWS), F32),
            jax.ShapeDtypeStruct((1, 1), F32),
        ),
        in_specs=[vmem],
        out_specs=(vmem, vmem, vmem),
    )(packed)
    return values.reshape(-1), targets.reshape(-1), loss.reshape(())


def solution(mesh):
    torus = Mesh(
        mesh.devices.reshape(DEPTHS, 4, 2, mesh.shape["head"]), SEQ + ("head",)
    )
    placed = (
        P(SEQ, None),
        P(None, "head"),
        P(None, "head"),
        P(),
        P(None, "head"),
        P("head"),
        P("head"),
        P("head"),
        P(None, "head"),
        P(),
        P("head"),
        P("head"),
        P(SEQ),
        P(SEQ),
        P(SEQ),
    )
    return jax.shard_map(
        per_device, mesh=torus, in_specs=placed, out_specs=(P(SEQ), P(SEQ), P()), check_vma=False
    )
```

```python
import functools

import jax
import jax.numpy as jnp
from jax import lax
from jax.experimental import pallas as pl
from jax.experimental.pallas import tpu as pltpu
from jax.sharding import Mesh
from jax.sharding import PartitionSpec as P

SEQ = ("seq_0", "seq_1", "seq_2")
MESH = pl.DeviceIdType.MESH
F32 = jnp.float32
BF16 = jnp.bfloat16

KCONV = 4
NSTEP = 8
DISCOUNT = 0.99
EXPECTILE = 0.7
EPSILON = 1e-05

HALO = 16
ROWS = 512
SPANS = ((0, 128), (128, 384))
LONGEST = 384
DEPTH = 2048
HEADS = 8
LANES = 128
WIDE = 256
TILE = 512
TILES = HEADS * LANES // TILE
TILE_HEADS = TILE // LANES
PLANE = 8
DEPTHS = 8
PEERS = 4


def silu(value):
    half = 0.5 * value
    return half + half * jnp.tanh(half)


def dot(a, b):
    return jnp.dot(a, b, preferred_element_type=F32)


def three_pieces(value):
    high = value.astype(BF16).astype(F32)
    rest = value - high
    middle = rest.astype(BF16).astype(F32)
    return high, middle, rest - middle


def down(row, rows=LANES):
    return jnp.broadcast_to(row, (rows, row.shape[1])).T


def kernel(
    seq_total,
    states,
    w_in,
    w_gate,
    w_state,
    w_step,
    bias_in,
    rate_in,
    skip_in,
    taps_in,
    taps_st,
    gain,
    weight,
    rewards,
    done,
    horizon,
    values_out,
    targets_out,
    loss_out,
    xs,
    wi,
    wg,
    ws,
    wt_in,
    bias,
    rate,
    skip,
    wt,
    tin,
    tst,
    gn,
    vw,
    rw,
    dn,
    hz,
    pre0,
    pre1,
    xh,
    ro,
    rdm,
    wtf,
    sc,
    lrow,
    dtrow,
    drow,
    tail,
    decb,
    recve1,
    dall,
    recve2,
    y,
    gs,
    send1,
    recv1,
    inside,
    reach_in,
    send2,
    recv2,
    send4,
    recv4,
    squares,
    valued_sum,
    held_values,
    held_targets,
    part,
    recvh,
    recvn,
    ext,
    recvr,
    coef,
    loss1,
    recvl,
    local_sem,
    tile_sem,
    near_sem,
    send_sem,
    recv_sem,
    s2,
    r2,
    r4,
    out_sem,
):
    z, x, c, head = (lax.axis_index(name) for name in SEQ + ("head",))
    here = x * 2 + c
    place = z * PLANE + here
    total = DEPTHS * PLANE
    after = lax.rem(place + 1, total)
    before = lax.rem(place + total - 1, total)

    def of_place(at, at_head):
        return (lax.div(at, PLANE), lax.div(lax.rem(at, PLANE), 2), lax.rem(at, 2), at_head)

    def in_plane(q):
        return (z, lax.div(q, 2), lax.rem(q, 2), head)

    def in_depth(k):
        return (k, x, c, head)

    def in_head(k):
        return (z, x, c, k)

    def put(src, dst, ssem, rsem, device):
        return pltpu.make_async_remote_copy(
            src_ref=src, dst_ref=dst, send_sem=ssem, recv_sem=rsem, device_id=device, device_id_type=MESH
        )

    def others(me, count, act):
        def one(i, carry):
            act(lax.rem(me + i, count))
            return carry

        lax.fori_loop(1, count, one, 0)

    def all_of(ref, count, which):
        whole = ref.at[pl.ds(0, count)]
        return put(whole, whole, send_sem.at[which], recv_sem.at[which], in_head(lax.rem(head + 1, PEERS)))

    small = [
        (states, xs.at[pl.ds(HALO, ROWS), :]),
        (w_step, wt_in),
        (bias_in, bias),
        (rate_in, rate),
        (skip_in, skip),
        (done, dn),
        (rewards, rw),
        (w_state, ws),
        (taps_st, tst),
        (taps_in, tin),
        (gain, gn),
        (weight, vw),
        (horizon, hz),
    ]
    local = [pltpu.make_async_copy(src, dst, local_sem.at[i]) for i, (src, dst) in enumerate(small)]

    def tile_copy(src, dst, slot, which):
        columns = pl.ds(pl.multiple_of(which * TILE, TILE), TILE)
        return pltpu.make_async_copy(src.at[:, columns], dst.at[which], tile_sem.at[slot, which])

    def turned(j):
        return lax.rem(j + x, TILES)

    for copy in local:
        copy.start()
    for j in range(TILES):
        tile_copy(w_in, wi, 0, turned(j)).start()

    barrier = pltpu.get_barrier_semaphore()

    def greet(device):
        pl.semaphore_signal(barrier, inc=1, device_id=device, device_id_type=MESH)

    others(z, DEPTHS, lambda k: greet(in_depth(k)))
    greet(of_place(before, head))
    for k in range(PEERS):
        greet(of_place(after, k))
    others(here, PLANE, lambda q: greet(in_plane(q)))
    others(head, PEERS, lambda k: greet(in_head(k)))

    local[5].wait()
    local[6].wait()
    alive = 1.0 - dn[...].astype(F32)
    ext[...] = jnp.zeros((8, ROWS + LANES), F32)
    ext[0:1, 0:ROWS] = rw[...]
    ext[1:2, 0:ROWS] = alive
    part[...] = jnp.zeros((8, ROWS), F32)
    local[1].wait()
    wt[...] = jnp.concatenate(
        [wt_in[...].astype(F32), jnp.zeros((LANES - HEADS, DEPTH), F32)], axis=0
    ).astype(BF16)
    local[0].wait()

    pl.semaphore_wait(barrier, (PLANE - 1) + (DEPTHS - 1) + (PEERS - 1) + 1 + PEERS)

    halo = put(
        states.at[pl.ds(ROWS - HALO, HALO), :],
        xs.at[pl.ds(0, HALO), :],
        near_sem.at[0],
        near_sem.at[1],
        of_place(after, head),
    )
    halo.start()
    rim = put(
        ext.at[:, pl.ds(0, LANES)], recvr, near_sem.at[2], near_sem.at[3], of_place(before, head)
    )
    rim.start()

    step_pre = lax.dot_general(
        xs[HALO : HALO + ROWS, :],
        wt[...],
        (((1,), (1,)), ((), ())),
        preferred_element_type=F32,
    ).T[0:HEADS, :]
    for i in (2, 3, 4):
        local[i].wait()
    order = lax.broadcasted_iota(jnp.int32, (HEADS, ROWS), 0)
    bias_rows = jnp.zeros((HEADS, ROWS), F32)
    rate_rows = jnp.zeros((HEADS, ROWS), F32)
    for h in range(HEADS):
        bias_rows = jnp.where(order == h, bias[h], bias_rows)
        rate_rows = jnp.where(order == h, rate[h], rate_rows)
    step_pre = step_pre + bias_rows
    step = jnp.maximum(step_pre, 0.0) + jnp.log1p(jnp.exp(-jnp.abs(step_pre)))
    dtrow[...] = step
    done_rows = jnp.broadcast_to(dn[...].astype(F32), (HEADS, ROWS))
    blocks = ROWS // LANES
    pieces = three_pieces(-(rate_rows * step)) + (done_rows,)
    stacked = jnp.concatenate(
        [p[:, b * LANES : (b + 1) * LANES] for p in pieces for b in range(blocks)], axis=0
    ).astype(BF16)
    triangle = (
        lax.broadcasted_iota(jnp.int32, (LANES, LANES), 0)
        <= lax.broadcasted_iota(jnp.int32, (LANES, LANES), 1)
    ).astype(F32).astype(BF16)
    sums = dot(stacked, triangle)
    span = HEADS * blocks
    decays = sums[0:span] + sums[span : 2 * span] + sums[2 * span : 3 * span]
    dones = sums[3 * span : 4 * span]

    def joined(parts):
        found, offset = [], jnp.zeros((HEADS, 1), F32)
        for b in range(blocks):
            block = parts[b * HEADS : (b + 1) * HEADS, :] + offset
            offset = block[:, LANES - 1 : LANES]
            found.append(block)
        return jnp.concatenate(found, axis=1), offset

    running, last = joined(decays)
    done_to, done_all = joined(dones)
    done_before = done_to - done_rows
    lrow[...] = running
    drow[...] = done_before
    tail[...] = jnp.where(done_before == done_all, jnp.exp(last - running) * step, 0.0)
    lost = jnp.broadcast_to(jnp.where(done_all == 0.0, jnp.exp(last), 0.0), (HEADS, LANES))
    decb[...] = lost
    others(
        here,
        PLANE,
        lambda q: put(decb, recve1.at[here], send_sem.at[0], recv_sem.at[0], in_plane(q)).start(),
    )
    recve1[here] = lost

    def convolved(pre, count, taps, columns):
        whole = pre[HALO : HALO + count, columns] * taps[KCONV - 1 : KCONV, :]
        for k in range(KCONV - 1):
            lag = KCONV - 1 - k
            whole = whole + pre[HALO - lag : HALO - lag + count, columns] * taps[k : k + 1, :]
        return silu(whole)

    def project(pre, part_of, tile):
        first, count = SPANS[part_of]
        rows = xs[first : first + HALO + count, :]
        if tile is None:
            pre[0 : HALO + count, 0:WIDE] = dot(rows, ws[...])
        else:
            pre[0 : HALO + count, :] = dot(rows, wi[tile])

    def finish(pre, part_of, tile):
        first, count = SPANS[part_of]
        rows = slice(first, first + count)
        if tile is None:
            wtf[:, rows] = convolved(pre, count, tst[:, 0:LANES], slice(0, LANES)).T
            ro[rows, :] = convolved(pre, count, tst[:, LANES:WIDE], slice(LANES, WIDE))
            return
        for k in range(TILE_HEADS):
            h = tile * TILE_HEADS + k
            taps = tin[:, pl.ds(pl.multiple_of(h * LANES, LANES), LANES)]
            conv = convolved(pre, count, taps, slice(k * LANES, (k + 1) * LANES))
            xh[h, rows, :] = conv.astype(BF16)

    def gained(tile):
        for k in range(TILE_HEADS):
            h = tile * TILE_HEADS + k
            added = dot((wtf[...] * tail[pl.ds(h, 1), :]).astype(BF16), xh[h])
            send1[h] = added.astype(BF16)

    def send_gained(tile):
        for k in range(TILE_HEADS):
            h = tile * TILE_HEADS + k

            @pl.when(h != here)
            def _():
                put(
                    send1.at[h], recv1.at[here], send_sem.at[1], recv_sem.at[1], in_plane(h)
                ).start()

    def gate_tile(j):
        tile_copy(w_gate, wg, 1, j).wait()
        gate = silu(dot(xs[HALO : HALO + ROWS, :], wg[j]))
        for k in range(TILE_HEADS):
            gs[j * TILE_HEADS + k] = gate[:, k * LANES : (k + 1) * LANES]

    pres = (pre0, pre1)
    tiles = [None] + [turned(j) for j in range(TILES)]

    for i in (7, 8, 9):
        local[i].wait()
    project(pres[0], 1, None)
    for i in range(1, TILES + 1):
        tile_copy(w_in, wi, 0, tiles[i]).wait()
        project(pres[i % 2], 1, tiles[i])
        finish(pres[(i - 1) % 2], 1, tiles[i - 1])
    for j in range(TILES):
        tile_copy(w_gate, wg, 1, j).start()
    finish(pres[TILES % 2], 1, tiles[TILES])

    halo.wait_recv()
    xs[0:HALO, :] = jnp.where(place > 0, xs[0:HALO, :].astype(F32), 0.0).astype(BF16)
    project(pres[0], 0, None)
    for i in range(1, TILES + 1):
        project(pres[i % 2], 0, tiles[i])
        finish(pres[(i - 1) % 2], 0, tiles[i - 1])
        if i > 1:
            gained(tiles[i - 1])
            send_gained(tiles[i - 1])
    finish(pres[TILES % 2], 0, tiles[TILES])
    gained(tiles[TILES])
    send_gained(tiles[TILES])

    all_of(recve1, PLANE - 1, 0).wait_recv()
    plane_lost = recve1[0]
    for q in range(1, PLANE):
        plane_lost = plane_lost * recve1[q]
    dall[...] = plane_lost
    others(
        z,
        DEPTHS,
        lambda k: put(dall, recve2.at[z], send_sem.at[2], recv_sem.at[2], in_depth(k)).start(),
    )
    recve2[z] = plane_lost
    recv1[here] = send1[here]

    for j in range(TILES):
        gate_tile(j)

    all_of(recv1, PLANE - 1, 1).wait_recv()

    def plane_step(q, carry):
        state, lasting = carry
        inside[q] = state
        reach_in[q] = jnp.broadcast_to(lasting, (8, LANES))
        lost = recve1[q, pl.ds(here, 1), :]
        return lost * state + recv1[q].astype(F32), lasting * lost

    state, _ = lax.fori_loop(
        0, PLANE, plane_step, (jnp.zeros((LANES, LANES), F32), jnp.ones((1, LANES), F32))
    )
    send2[...] = state.astype(BF16)

    def to_later(k):
        return put(send2, recv2.at[z], s2.at[k], r2.at[z], in_depth(k))

    def later(act):
        def one(k, carry):
            act(k)
            return carry

        lax.fori_loop(z + 1, DEPTHS, one, 0)

    later(lambda k: to_later(k).start())

    done_row = drow[0:1, :]
    done_down = down(done_row)
    rdm[...] = jnp.where(done_down == 0.0, ro[...], 0.0).astype(BF16)
    readout = ro[...].astype(BF16)
    writes_t = wtf[...].astype(BF16)
    for b in range(2):
        rows = slice(b * WIDE, (b + 1) * WIDE)
        upto = (b + 1) * WIDE
        scores = dot(readout[rows, :], writes_t[:, 0:upto])
        at_row = lax.broadcasted_iota(jnp.int32, (WIDE, LANES), 0) + b * WIDE
        for k in range(upto // LANES):
            columns = slice(k * LANES, (k + 1) * LANES)
            at_column = lax.broadcasted_iota(jnp.int32, (WIDE, LANES), 1) + k * LANES
            seen = (at_row >= at_column) & (done_down[rows, :] == done_row[:, columns])
            sc[rows, columns] = jnp.where(seen, scores[:, columns], 0.0)

    def own_scan(h, carry):
        across = lrow[pl.ds(h, 1), :]
        step_across = dtrow[pl.ds(h, 1), :]
        along = down(across)
        inner = xh[h]
        for b in range(2):
            rows = slice(b * WIDE, (b + 1) * WIDE)
            upto = (b + 1) * WIDE
            weights = []
            for k in range(upto // LANES):
                columns = slice(k * LANES, (k + 1) * LANES)
                gap = jnp.minimum(along[rows, :] - across[:, columns], 0.0)
                weights.append((jnp.exp(gap) * step_across[:, columns] * sc[rows, columns]).astype(BF16))
            mixed = dot(jnp.concatenate(weights, axis=1), inner[0:upto, :])
            y[h, rows, :] = (mixed + skip[h] * inner[rows, :].astype(F32)) * gs[h, rows, :]
        gs[h] = jnp.exp(along) * gs[h]
        return carry

    lax.fori_loop(0, HEADS - 2, own_scan, 0)

    all_of(recve2, DEPTHS - 1, 2).wait_recv()

    def depth_step(k, state):
        put(send2, recv2.at[k], s2.at[k], r2.at[k], in_depth(k)).wait_recv()
        return recve2[k, pl.ds(here, 1), :] * state + recv2[k].astype(F32)

    entering = lax.fori_loop(0, z, depth_step, jnp.zeros((LANES, LANES), F32))

    def carried(q):
        send4[q] = (reach_in[q][0:1, :] * entering + inside[q]).astype(BF16)

    def hand_out(q):
        carried(q)
        put(send4.at[q], recv4.at[here], send_sem.at[3], r4.at[here], in_plane(q)).start()

    others(here, PLANE, hand_out)
    carried(here)
    recv4[here] = send4[here]

    lax.fori_loop(HEADS - 2, HEADS, own_scan, 0)

    for i in (10, 11, 12):
        local[i].wait()
    rim.wait_recv()
    is_last = place == total - 1
    ext[:, ROWS : ROWS + LANES] = jnp.where(is_last, 0.0, recvr[...])
    length = ROWS + LANES
    survive = jnp.ones((1, ROWS), F32)
    rewarded = jnp.zeros((1, ROWS), F32)
    for k in range(NSTEP + 1):
        ahead = ext[...] if k == 0 else pltpu.roll(ext[...], length - k, 1)
        factor = DISCOUNT**k * survive
        rewarded = rewarded + jnp.where(k < hz[...], factor * ahead[0:1, 0:ROWS], 0.0)
        coef[k : k + 1, :] = jnp.where(k == hz[...], factor, 0.0)
        survive = survive * ahead[1:2, 0:ROWS]
    coef[NSTEP + 1 : NSTEP + 2, :] = rewarded
    gn[...] = gn[...] * vw[...]

    def mix(h):
        gated = y[h] + dot(rdm[...], recv4[h]) * gs[h]
        scale = gn[:, pl.ds(pl.multiple_of(h * LANES, LANES), LANES)]
        return gated * gated, gated * scale

    squares[...], valued_sum[...] = mix(here)

    def mix_arrived(i, carry):
        h = lax.rem(here + PLANE - i, PLANE)
        put(send4.at[h], recv4.at[h], send_sem.at[3], r4.at[h], in_plane(h)).wait_recv()
        more_squares, more_valued = mix(h)
        squares[...] = squares[...] + more_squares
        valued_sum[...] = valued_sum[...] + more_valued
        return carry

    lax.fori_loop(1, PLANE, mix_arrived, 0)
    part[0:1, :] = jnp.sum(squares[...].T, axis=0, keepdims=True)
    part[1:2, :] = jnp.sum(valued_sum[...].T, axis=0, keepdims=True)

    def to_before(k):
        return put(
            part.at[:, pl.ds(0, LANES)],
            recvn.at[head],
            send_sem.at[5],
            recv_sem.at[5],
            of_place(before, k),
        )

    for k in range(PEERS):
        to_before(k).start()
    others(
        head,
        PEERS,
        lambda k: put(part, recvh.at[head], send_sem.at[4], recv_sem.at[4], in_head(k)).start(),
    )
    recvh[head] = part[...]
    all_of(recvh, PEERS - 1, 4).wait_recv()
    all_of(recvn, PEERS, 5).wait_recv()

    def normed(sums):
        return sums[1:2, :] * lax.rsqrt(sums[0:1, :] / (PEERS * HEADS * LANES) + EPSILON)

    own = normed(recvh[0] + recvh[1] + recvh[2] + recvh[3])
    following = normed(recvn[0] + recvn[1] + recvn[2] + recvn[3])
    following = jnp.where(is_last, 0.0, following)
    valued = jnp.broadcast_to(jnp.concatenate([own, following], axis=1), (8, length))
    targets = coef[NSTEP + 1 : NSTEP + 2, :]
    for k in range(NSTEP + 1):
        ahead = valued if k == 0 else pltpu.roll(valued, length - k, 1)
        targets = targets + coef[k : k + 1, :] * ahead[0:1, 0:ROWS]
    residual = targets - own
    terms = jnp.where(residual < 0, 1.0 - EXPECTILE, EXPECTILE) * residual * residual
    mine = jnp.broadcast_to(jnp.sum(terms, axis=1, keepdims=True), (1, LANES))
    loss1[...] = mine

    def tell(device):
        put(loss1, recvl.at[place], send_sem.at[6], recv_sem.at[6], device).start()

    def tell_plane(k):
        for q in range(PLANE):
            tell((k, q // 2, q % 2, head))

    others(z, DEPTHS, tell_plane)
    others(here, PLANE, lambda q: tell(in_plane(q)))
    recvl[place] = mine
    held_values[...] = own
    held_targets[...] = targets
    written = [
        pltpu.make_async_copy(held_values, values_out, out_sem.at[0]),
        pltpu.make_async_copy(held_targets, targets_out, out_sem.at[1]),
    ]
    for copy in written:
        copy.start()

    halo.wait_send()
    rim.wait_send()
    all_of(recve1, PLANE - 1, 0).wait_send()
    all_of(recv1, PLANE - 1, 1).wait_send()
    all_of(recve2, DEPTHS - 1, 2).wait_send()
    all_of(recv4, PLANE - 1, 3).wait_send()
    all_of(recvh, PEERS - 1, 4).wait_send()
    all_of(recvn, PEERS, 5).wait_send()
    later(lambda k: to_later(k).wait_send())

    all_of(recvl, total - 1, 6).wait_recv()
    loss_out[...] = (jnp.sum(recvl[...], axis=0) / seq_total)[:, 0:1]
    for copy in written:
        copy.wait()
    all_of(recvl, total - 1, 6).wait_send()


def hand_over(values, targets, loss, values_out, targets_out, loss_out, sem):
    pairs = ((values, values_out), (targets, targets_out), (loss, loss_out))
    copies = [pltpu.make_async_copy(src, dst, sem.at[i]) for i, (src, dst) in enumerate(pairs)]
    for copy in copies:
        copy.start()
    for copy in copies:
        copy.wait()


def scratch():
    v = pltpu.VMEM
    dma = pltpu.SemaphoreType.DMA
    return [
        v((HALO + ROWS, DEPTH), BF16),
        v((TILES, DEPTH, TILE), BF16),
        v((TILES, DEPTH, TILE), BF16),
        v((DEPTH, WIDE), BF16),
        v((HEADS, DEPTH), BF16),
        pltpu.SMEM((HEADS,), F32),
        pltpu.SMEM((HEADS,), F32),
        pltpu.SMEM((HEADS,), F32),
        v((LANES, DEPTH), BF16),
        v((KCONV, HEADS * LANES), F32),
        v((KCONV, WIDE), F32),
        v((1, HEADS * LANES), F32),
        v((1, HEADS * LANES), F32),
        v((1, ROWS), F32),
        v((1, ROWS), jnp.int32),
        v((1, ROWS), jnp.int32),
        v((HALO + LONGEST, TILE), F32),
        v((HALO + LONGEST, TILE), F32),
        v((HEADS, ROWS, LANES), BF16),
        v((ROWS, LANES), F32),
        v((ROWS, LANES), BF16),
        v((LANES, ROWS), F32),
        v((ROWS, ROWS), F32),
        v((HEADS, ROWS), F32),
        v((HEADS, ROWS), F32),
        v((HEADS, ROWS), F32),
        v((HEADS, ROWS), F32),
        v((HEADS, LANES), F32),
        v((PLANE, HEADS, LANES), F32),
        v((HEADS, LANES), F32),
        v((DEPTHS, HEADS, LANES), F32),
        v((HEADS, ROWS, LANES), F32),
        v((HEADS, ROWS, LANES), F32),
        v((PLANE, LANES, LANES), BF16),
        v((PLANE, LANES, LANES), BF16),
        v((PLANE, LANES, LANES), F32),
        v((PLANE, 8, LANES), F32),
        v((LANES, LANES), BF16),
        v((DEPTHS, LANES, LANES), BF16),
        v((PLANE, LANES, LANES), BF16),
        v((PLANE, LANES, LANES), BF16),
        v((ROWS, LANES), F32),
        v((ROWS, LANES), F32),
        v((1, ROWS), F32),
        v((1, ROWS), F32),
        v((8, ROWS), F32),
        v((PEERS, 8, ROWS), F32),
        v((PEERS, 8, LANES), F32),
        v((8, ROWS + LANES), F32),
        v((8, LANES), F32),
        v((16, ROWS), F32),
        v((1, LANES), F32),
        v((DEPTHS * PLANE, 1, LANES), F32),
        dma((13,)),
        dma((2, TILES)),
        dma((4,)),
        dma((7,)),
        dma((7,)),
        dma((DEPTHS,)),
        dma((DEPTHS,)),
        dma((PLANE,)),
        dma((2,)),
    ]


def per_device(
    states,
    inner_weight,
    gate_weight,
    state_weight,
    step_weight,
    step_bias,
    decay_rate,
    skip_gain,
    conv_inner,
    conv_state,
    norm_gain,
    value_weight,
    rewards,
    done_flags,
    horizon,
):
    hbm = pl.BlockSpec(memory_space=pl.ANY)
    vmem = pl.BlockSpec(memory_space=pltpu.VMEM)
    seq_total = states.shape[0] * DEPTHS * PLANE
    results = (
        jax.ShapeDtypeStruct((1, ROWS), F32),
        jax.ShapeDtypeStruct((1, ROWS), F32),
        jax.ShapeDtypeStruct((1, 1), F32),
    )
    found = pl.pallas_call(
        functools.partial(kernel, seq_total),
        out_shape=results,
        in_specs=[hbm] * 15,
        out_specs=(hbm, hbm, vmem),
        scratch_shapes=scratch(),
        compiler_params=pltpu.CompilerParams(
            collective_id=0, has_side_effects=True, vmem_limit_bytes=56 * 2**20
        ),
    )(
        states,
        inner_weight,
        gate_weight,
        state_weight,
        step_weight.T,
        step_bias,
        decay_rate,
        skip_gain,
        conv_inner,
        conv_state,
        norm_gain.reshape(1, -1),
        value_weight.reshape(1, -1),
        rewards.reshape(1, -1),
        done_flags.reshape(1, -1),
        horizon.reshape(1, -1),
    )
    values, targets, loss = pl.pallas_call(
        hand_over,
        out_shape=results,
        in_specs=[hbm] * 3,
        out_specs=(hbm, hbm, hbm),
        scratch_shapes=[pltpu.SemaphoreType.DMA((3,))],
    )(*found)
    return values.reshape(-1), targets.reshape(-1), loss.reshape(())


def solution(mesh):
    torus = Mesh(
        mesh.devices.reshape(DEPTHS, 4, 2, mesh.shape["head"]), SEQ + ("head",)
    )
    placed = (
        P(SEQ, None),
        P(None, "head"),
        P(None, "head"),
        P(),
        P(None, "head"),
        P("head"),
        P("head"),
        P("head"),
        P(None, "head"),
        P(),
        P("head"),
        P("head"),
        P(SEQ),
        P(SEQ),
        P(SEQ),
    )
    return jax.shard_map(
        per_device, mesh=torus, in_specs=placed, out_specs=(P(SEQ), P(SEQ), P()), check_vma=False
    )
```

```python
import functools

import jax
import jax.numpy as jnp
from jax import lax
from jax.experimental import pallas as pl
from jax.experimental.pallas import tpu as pltpu
from jax.sharding import Mesh
from jax.sharding import PartitionSpec as P

SEQ = ("seq_0", "seq_1", "seq_2")
MESH = pl.DeviceIdType.MESH
F32 = jnp.float32
BF16 = jnp.bfloat16

KCONV = 4
NSTEP = 8
DISCOUNT = 0.99
EXPECTILE = 0.7
EPSILON = 1e-05

HALO = 16
ROWS = 512
SPANS = ((0, 128), (128, 384))
LONGEST = 384
DEPTH = 2048
HEADS = 8
LANES = 128
WIDE = 256
TILE = 512
TILES = HEADS * LANES // TILE
TILE_HEADS = TILE // LANES
PLANE = 8
DEPTHS = 8
PEERS = 4


def silu(value):
    half = 0.5 * value
    return half + half * jnp.tanh(half)


def dot(a, b):
    return jnp.dot(a, b, preferred_element_type=F32)


def three_pieces(value):
    high = value.astype(BF16).astype(F32)
    rest = value - high
    middle = rest.astype(BF16).astype(F32)
    return high, middle, rest - middle


def down(row, rows=LANES):
    return jnp.broadcast_to(row, (rows, row.shape[1])).T


def kernel(
    seq_total,
    states,
    w_in,
    w_gate,
    w_state,
    w_step,
    bias_in,
    rate_in,
    skip_in,
    taps_in,
    taps_st,
    gain,
    weight,
    rewards,
    done,
    horizon,
    out,
    xs,
    wi,
    wg,
    ws,
    wt_in,
    bias,
    rate,
    skip,
    wt,
    tin,
    tst,
    gn,
    vw,
    rw,
    dn,
    hz,
    pre0,
    pre1,
    xh,
    ro,
    rdm,
    wtf,
    sc,
    lrow,
    dtrow,
    drow,
    tail,
    decb,
    recve1,
    dall,
    recve2,
    y,
    gs,
    send1,
    recv1,
    inside,
    reach_in,
    send2,
    recv2,
    send4,
    recv4,
    squares,
    valued_sum,
    part,
    recvh,
    recvn,
    ext,
    recvr,
    coef,
    loss1,
    recvl,
    local_sem,
    tile_sem,
    near_sem,
    send_sem,
    recv_sem,
    s2,
    r2,
    r4,
):
    z, x, c, head = (lax.axis_index(name) for name in SEQ + ("head",))
    here = x * 2 + c
    place = z * PLANE + here
    total = DEPTHS * PLANE
    after = lax.rem(place + 1, total)
    before = lax.rem(place + total - 1, total)

    def of_place(at, at_head):
        return (lax.div(at, PLANE), lax.div(lax.rem(at, PLANE), 2), lax.rem(at, 2), at_head)

    def in_plane(q):
        return (z, lax.div(q, 2), lax.rem(q, 2), head)

    def in_depth(k):
        return (k, x, c, head)

    def in_head(k):
        return (z, x, c, k)

    def put(src, dst, ssem, rsem, device):
        return pltpu.make_async_remote_copy(
            src_ref=src, dst_ref=dst, send_sem=ssem, recv_sem=rsem, device_id=device, device_id_type=MESH
        )

    def others(me, count, act):
        def one(i, carry):
            act(lax.rem(me + i, count))
            return carry

        lax.fori_loop(1, count, one, 0)

    def all_of(ref, count, which):
        whole = ref.at[pl.ds(0, count)]
        return put(whole, whole, send_sem.at[which], recv_sem.at[which], in_head(lax.rem(head + 1, PEERS)))

    small = [
        (states, xs.at[pl.ds(HALO, ROWS), :]),
        (w_step, wt_in),
        (bias_in, bias),
        (rate_in, rate),
        (skip_in, skip),
        (done, dn),
        (rewards, rw),
        (w_state, ws),
        (taps_st, tst),
        (taps_in, tin),
        (gain, gn),
        (weight, vw),
        (horizon, hz),
    ]
    local = [pltpu.make_async_copy(src, dst, local_sem.at[i]) for i, (src, dst) in enumerate(small)]

    def tile_copy(src, dst, slot, which):
        columns = pl.ds(pl.multiple_of(which * TILE, TILE), TILE)
        return pltpu.make_async_copy(src.at[:, columns], dst.at[which], tile_sem.at[slot, which])

    def turned(j):
        return lax.rem(j + x, TILES)

    for i in (0, 1, 5, 6, 2, 3, 4, 8, 9, 7):
        local[i].start()

    barrier = pltpu.get_barrier_semaphore()

    def greet(device):
        pl.semaphore_signal(barrier, inc=1, device_id=device, device_id_type=MESH)

    others(z, DEPTHS, lambda k: greet(in_depth(k)))
    tile_copy(w_in, wi, 0, turned(0)).start()
    greet(of_place(before, head))
    for k in range(PEERS):
        greet(of_place(after, k))
    others(here, PLANE, lambda q: greet(in_plane(q)))
    others(head, PEERS, lambda k: greet(in_head(k)))
    tile_copy(w_in, wi, 0, turned(1)).start()

    local[5].wait()
    local[6].wait()
    alive = 1.0 - dn[...].astype(F32)
    ext[...] = jnp.zeros((8, ROWS + LANES), F32)
    ext[0:1, 0:ROWS] = rw[...]
    ext[1:2, 0:ROWS] = alive
    part[...] = jnp.zeros((8, ROWS), F32)
    local[1].wait()
    wt[...] = jnp.concatenate(
        [wt_in[...].astype(F32), jnp.zeros((LANES - HEADS, DEPTH), F32)], axis=0
    ).astype(BF16)
    local[0].wait()
    pl.semaphore_wait(barrier, (PLANE - 1) + (DEPTHS - 1) + (PEERS - 1) + 1 + PEERS)

    halo = put(
        states.at[pl.ds(ROWS - HALO, HALO), :],
        xs.at[pl.ds(0, HALO), :],
        near_sem.at[0],
        near_sem.at[1],
        of_place(after, head),
    )
    halo.start()
    rim = put(
        ext.at[:, pl.ds(0, LANES)], recvr, near_sem.at[2], near_sem.at[3], of_place(before, head)
    )
    rim.start()

    step_pre = lax.dot_general(
        xs[HALO : HALO + ROWS, :],
        wt[...],
        (((1,), (1,)), ((), ())),
        preferred_element_type=F32,
    ).T[0:HEADS, :]
    for i in (2, 3, 4):
        local[i].wait()
    order = lax.broadcasted_iota(jnp.int32, (HEADS, ROWS), 0)
    bias_rows = jnp.zeros((HEADS, ROWS), F32)
    rate_rows = jnp.zeros((HEADS, ROWS), F32)
    for h in range(HEADS):
        bias_rows = jnp.where(order == h, bias[h], bias_rows)
        rate_rows = jnp.where(order == h, rate[h], rate_rows)
    step_pre = step_pre + bias_rows
    step = jnp.maximum(step_pre, 0.0) + jnp.log1p(jnp.exp(-jnp.abs(step_pre)))
    dtrow[...] = step
    done_rows = jnp.broadcast_to(dn[...].astype(F32), (HEADS, ROWS))
    blocks = ROWS // LANES
    pieces = three_pieces(-(rate_rows * step)) + (done_rows,)
    stacked = jnp.concatenate(
        [p[:, b * LANES : (b + 1) * LANES] for p in pieces for b in range(blocks)], axis=0
    ).astype(BF16)
    triangle = (
        lax.broadcasted_iota(jnp.int32, (LANES, LANES), 0)
        <= lax.broadcasted_iota(jnp.int32, (LANES, LANES), 1)
    ).astype(F32).astype(BF16)
    sums = dot(stacked, triangle)
    span = HEADS * blocks
    decays = sums[0:span] + sums[span : 2 * span] + sums[2 * span : 3 * span]
    dones = sums[3 * span : 4 * span]

    def joined(parts):
        found, offset = [], jnp.zeros((HEADS, 1), F32)
        for b in range(blocks):
            block = parts[b * HEADS : (b + 1) * HEADS, :] + offset
            offset = block[:, LANES - 1 : LANES]
            found.append(block)
        return jnp.concatenate(found, axis=1), offset

    running, last = joined(decays)
    done_to, done_all = joined(dones)
    done_before = done_to - done_rows
    lrow[...] = running
    drow[...] = done_before
    tail[...] = jnp.where(done_before == done_all, jnp.exp(last - running) * step, 0.0)
    lost = jnp.broadcast_to(jnp.where(done_all == 0.0, jnp.exp(last), 0.0), (HEADS, LANES))
    decb[...] = lost
    others(
        here,
        PLANE,
        lambda q: put(decb, recve1.at[here], send_sem.at[0], recv_sem.at[0], in_plane(q)).start(),
    )
    recve1[here] = lost

    def convolved(pre, count, taps, columns):
        whole = pre[HALO : HALO + count, columns] * taps[KCONV - 1 : KCONV, :]
        for k in range(KCONV - 1):
            lag = KCONV - 1 - k
            whole = whole + pre[HALO - lag : HALO - lag + count, columns] * taps[k : k + 1, :]
        return silu(whole)

    def project(pre, part_of, tile):
        first, count = SPANS[part_of]
        rows = xs[first : first + HALO + count, :]
        if tile is None:
            pre[0 : HALO + count, 0:WIDE] = dot(rows, ws[...])
        else:
            pre[0 : HALO + count, :] = dot(rows, wi[tile])

    def finish(pre, part_of, tile):
        first, count = SPANS[part_of]
        rows = slice(first, first + count)
        if tile is None:
            wtf[:, rows] = convolved(pre, count, tst[:, 0:LANES], slice(0, LANES)).T
            ro[rows, :] = convolved(pre, count, tst[:, LANES:WIDE], slice(LANES, WIDE))
            return
        for k in range(TILE_HEADS):
            h = tile * TILE_HEADS + k
            taps = tin[:, pl.ds(pl.multiple_of(h * LANES, LANES), LANES)]
            conv = convolved(pre, count, taps, slice(k * LANES, (k + 1) * LANES))
            xh[h, rows, :] = conv.astype(BF16)

    def gained(tile):
        for k in range(TILE_HEADS):
            h = tile * TILE_HEADS + k
            added = dot((wtf[...] * tail[pl.ds(h, 1), :]).astype(BF16), xh[h])
            send1[h] = added.astype(BF16)

    def send_gained(tile):
        for k in range(TILE_HEADS):
            h = tile * TILE_HEADS + k

            @pl.when(h != here)
            def _():
                put(
                    send1.at[h], recv1.at[here], send_sem.at[1], recv_sem.at[1], in_plane(h)
                ).start()

    def gate_tile(j):
        tile_copy(w_gate, wg, 1, j).wait()
        gate = silu(dot(xs[HALO : HALO + ROWS, :], wg[j]))
        for k in range(TILE_HEADS):
            gs[j * TILE_HEADS + k] = gate[:, k * LANES : (k + 1) * LANES]

    pres = (pre0, pre1)
    tiles = [None] + [turned(j) for j in range(TILES)]

    for i in (7, 8, 9):
        local[i].wait()
    project(pres[0], 1, None)
    for i in range(1, TILES + 1):
        tile_copy(w_in, wi, 0, tiles[i]).wait()
        project(pres[i % 2], 1, tiles[i])
        finish(pres[(i - 1) % 2], 1, tiles[i - 1])
    for j in range(TILES):
        tile_copy(w_gate, wg, 1, j).start()
    for i in (10, 11, 12):
        local[i].start()
    finish(pres[TILES % 2], 1, tiles[TILES])

    halo.wait_recv()
    xs[0:HALO, :] = jnp.where(place > 0, xs[0:HALO, :].astype(F32), 0.0).astype(BF16)
    project(pres[0], 0, None)
    for i in range(1, TILES + 1):
        project(pres[i % 2], 0, tiles[i])
        finish(pres[(i - 1) % 2], 0, tiles[i - 1])
        if i > 1:
            gained(tiles[i - 1])
            send_gained(tiles[i - 1])
    finish(pres[TILES % 2], 0, tiles[TILES])
    gained(tiles[TILES])
    send_gained(tiles[TILES])

    all_of(recve1, PLANE - 1, 0).wait_recv()
    plane_lost = recve1[0]
    for q in range(1, PLANE):
        plane_lost = plane_lost * recve1[q]
    dall[...] = plane_lost
    others(
        z,
        DEPTHS,
        lambda k: put(dall, recve2.at[z], send_sem.at[2], recv_sem.at[2], in_depth(k)).start(),
    )
    recve2[z] = plane_lost
    recv1[here] = send1[here]

    for j in range(TILES):
        gate_tile(j)

    all_of(recv1, PLANE - 1, 1).wait_recv()

    def plane_step(q, carry):
        state, lasting = carry
        inside[q] = state
        reach_in[q] = jnp.broadcast_to(lasting, (8, LANES))
        lost = recve1[q, pl.ds(here, 1), :]
        return lost * state + recv1[q].astype(F32), lasting * lost

    state, _ = lax.fori_loop(
        0, PLANE, plane_step, (jnp.zeros((LANES, LANES), F32), jnp.ones((1, LANES), F32))
    )
    send2[...] = state.astype(BF16)

    def to_later(k):
        return put(send2, recv2.at[z], s2.at[k], r2.at[z], in_depth(k))

    def later(act):
        def one(k, carry):
            act(k)
            return carry

        lax.fori_loop(z + 1, DEPTHS, one, 0)

    later(lambda k: to_later(k).start())

    done_row = drow[0:1, :]
    done_down = down(done_row)
    rdm[...] = jnp.where(done_down == 0.0, ro[...], 0.0).astype(BF16)
    readout = ro[...].astype(BF16)
    writes_t = wtf[...].astype(BF16)
    for b in range(2):
        rows = slice(b * WIDE, (b + 1) * WIDE)
        upto = (b + 1) * WIDE
        scores = dot(readout[rows, :], writes_t[:, 0:upto])
        at_row = lax.broadcasted_iota(jnp.int32, (WIDE, LANES), 0) + b * WIDE
        for k in range(upto // LANES):
            columns = slice(k * LANES, (k + 1) * LANES)
            at_column = lax.broadcasted_iota(jnp.int32, (WIDE, LANES), 1) + k * LANES
            seen = (at_row >= at_column) & (done_down[rows, :] == done_row[:, columns])
            sc[rows, columns] = jnp.where(seen, scores[:, columns], 0.0)

    def own_scan(h, carry):
        across = lrow[pl.ds(h, 1), :]
        step_across = dtrow[pl.ds(h, 1), :]
        along = down(across)
        inner = xh[h]
        for b in range(2):
            rows = slice(b * WIDE, (b + 1) * WIDE)
            upto = (b + 1) * WIDE
            weights = []
            for k in range(upto // LANES):
                columns = slice(k * LANES, (k + 1) * LANES)
                gap = jnp.minimum(along[rows, :] - across[:, columns], 0.0)
                weights.append((jnp.exp(gap) * step_across[:, columns] * sc[rows, columns]).astype(BF16))
            mixed = dot(jnp.concatenate(weights, axis=1), inner[0:upto, :])
            y[h, rows, :] = (mixed + skip[h] * inner[rows, :].astype(F32)) * gs[h, rows, :]
        gs[h] = jnp.exp(along) * gs[h]
        return carry

    lax.fori_loop(0, HEADS - 2, own_scan, 0)

    all_of(recve2, DEPTHS - 1, 2).wait_recv()

    def depth_step(k, state):
        put(send2, recv2.at[k], s2.at[k], r2.at[k], in_depth(k)).wait_recv()
        return recve2[k, pl.ds(here, 1), :] * state + recv2[k].astype(F32)

    entering = lax.fori_loop(0, z, depth_step, jnp.zeros((LANES, LANES), F32))

    def carried(q):
        send4[q] = (reach_in[q][0:1, :] * entering + inside[q]).astype(BF16)

    def hand_out(q):
        carried(q)
        put(send4.at[q], recv4.at[here], send_sem.at[3], r4.at[here], in_plane(q)).start()

    others(here, PLANE, hand_out)
    carried(here)
    recv4[here] = send4[here]

    lax.fori_loop(HEADS - 2, HEADS, own_scan, 0)

    for i in (10, 11, 12):
        local[i].wait()
    rim.wait_recv()
    is_last = place == total - 1
    ext[:, ROWS : ROWS + LANES] = jnp.where(is_last, 0.0, recvr[...])
    length = ROWS + LANES
    survive = jnp.ones((1, ROWS), F32)
    rewarded = jnp.zeros((1, ROWS), F32)
    for k in range(NSTEP + 1):
        ahead = ext[...] if k == 0 else pltpu.roll(ext[...], length - k, 1)
        factor = DISCOUNT**k * survive
        rewarded = rewarded + jnp.where(k < hz[...], factor * ahead[0:1, 0:ROWS], 0.0)
        coef[k : k + 1, :] = jnp.where(k == hz[...], factor, 0.0)
        survive = survive * ahead[1:2, 0:ROWS]
    coef[NSTEP + 1 : NSTEP + 2, :] = rewarded
    gn[...] = gn[...] * vw[...]

    def mix(h):
        gated = y[h] + dot(rdm[...], recv4[h]) * gs[h]
        scale = gn[:, pl.ds(pl.multiple_of(h * LANES, LANES), LANES)]
        return gated * gated, gated * scale

    squares[...], valued_sum[...] = mix(here)

    def mix_arrived(i, carry):
        h = lax.rem(here + PLANE - i, PLANE)
        put(send4.at[h], recv4.at[h], send_sem.at[3], r4.at[h], in_plane(h)).wait_recv()
        more_squares, more_valued = mix(h)
        squares[...] = squares[...] + more_squares
        valued_sum[...] = valued_sum[...] + more_valued
        return carry

    lax.fori_loop(1, PLANE, mix_arrived, 0)

    def to_before(k):
        return put(
            part.at[:, pl.ds(0, LANES)],
            recvn.at[head],
            send_sem.at[5],
            recv_sem.at[5],
            of_place(before, k),
        )

    for first, past in ((0, LANES), (LANES, ROWS)):
        part[0:1, first:past] = jnp.sum(squares[first:past, :].T, axis=0, keepdims=True)
        part[1:2, first:past] = jnp.sum(valued_sum[first:past, :].T, axis=0, keepdims=True)
        if first == 0:
            for k in range(PEERS):
                to_before(k).start()
    others(
        head,
        PEERS,
        lambda k: put(part, recvh.at[head], send_sem.at[4], recv_sem.at[4], in_head(k)).start(),
    )
    recvh[head] = part[...]
    all_of(recvh, PEERS - 1, 4).wait_recv()
    all_of(recvn, PEERS, 5).wait_recv()

    def normed(sums):
        return sums[1:2, :] * lax.rsqrt(sums[0:1, :] / (PEERS * HEADS * LANES) + EPSILON)

    own = normed(recvh[0] + recvh[1] + recvh[2] + recvh[3])
    following = normed(recvn[0] + recvn[1] + recvn[2] + recvn[3])
    following = jnp.where(is_last, 0.0, following)
    valued = jnp.broadcast_to(jnp.concatenate([own, following], axis=1), (8, length))
    targets = coef[NSTEP + 1 : NSTEP + 2, :]
    for k in range(NSTEP + 1):
        ahead = valued if k == 0 else pltpu.roll(valued, length - k, 1)
        targets = targets + coef[k : k + 1, :] * ahead[0:1, 0:ROWS]
    residual = targets - own
    terms = jnp.where(residual < 0, 1.0 - EXPECTILE, EXPECTILE) * residual * residual
    mine = jnp.broadcast_to(jnp.sum(terms, axis=1, keepdims=True), (1, LANES))
    loss1[...] = mine

    def tell(device):
        put(loss1, recvl.at[place], send_sem.at[6], recv_sem.at[6], device).start()

    def tell_plane(k):
        for q in range(PLANE):
            tell((k, q // 2, q % 2, head))

    def tell_planes(first, past):
        def one(k, carry):
            tell_plane(k)
            return carry

        lax.fori_loop(first, past, one, 0)

    tell_planes(0, z)
    tell_planes(z + 1, DEPTHS)
    others(here, PLANE, lambda q: tell(in_plane(q)))
    recvl[place] = mine
    out[0:1, :] = own
    out[1:2, :] = targets

    halo.wait_send()
    rim.wait_send()
    all_of(recve1, PLANE - 1, 0).wait_send()
    all_of(recv1, PLANE - 1, 1).wait_send()
    all_of(recve2, DEPTHS - 1, 2).wait_send()
    all_of(recv4, PLANE - 1, 3).wait_send()
    all_of(recvh, PEERS - 1, 4).wait_send()
    all_of(recvn, PEERS, 5).wait_send()
    later(lambda k: to_later(k).wait_send())

    all_of(recvl, total - 1, 6).wait_recv()
    out[2:3, 0:LANES] = jnp.sum(recvl[...], axis=0) / seq_total
    all_of(recvl, total - 1, 6).wait_send()


def unpack(packed, values, targets, loss):
    values[...] = packed[0:1, :]
    targets[...] = packed[1:2, :]
    loss[...] = packed[2:3, 0:1]


def scratch():
    v = pltpu.VMEM
    dma = pltpu.SemaphoreType.DMA
    return [
        v((HALO + ROWS, DEPTH), BF16),
        v((TILES, DEPTH, TILE), BF16),
        v((TILES, DEPTH, TILE), BF16),
        v((DEPTH, WIDE), BF16),
        v((HEADS, DEPTH), BF16),
        pltpu.SMEM((HEADS,), F32),
        pltpu.SMEM((HEADS,), F32),
        pltpu.SMEM((HEADS,), F32),
        v((LANES, DEPTH), BF16),
        v((KCONV, HEADS * LANES), F32),
        v((KCONV, WIDE), F32),
        v((1, HEADS * LANES), F32),
        v((1, HEADS * LANES), F32),
        v((1, ROWS), F32),
        v((1, ROWS), jnp.int32),
        v((1, ROWS), jnp.int32),
        v((HALO + LONGEST, TILE), F32),
        v((HALO + LONGEST, TILE), F32),
        v((HEADS, ROWS, LANES), BF16),
        v((ROWS, LANES), F32),
        v((ROWS, LANES), BF16),
        v((LANES, ROWS), F32),
        v((ROWS, ROWS), F32),
        v((HEADS, ROWS), F32),
        v((HEADS, ROWS), F32),
        v((HEADS, ROWS), F32),
        v((HEADS, ROWS), F32),
        v((HEADS, LANES), F32),
        v((PLANE, HEADS, LANES), F32),
        v((HEADS, LANES), F32),
        v((DEPTHS, HEADS, LANES), F32),
        v((HEADS, ROWS, LANES), F32),
        v((HEADS, ROWS, LANES), F32),
        v((PLANE, LANES, LANES), BF16),
        v((PLANE, LANES, LANES), BF16),
        v((PLANE, LANES, LANES), F32),
        v((PLANE, 8, LANES), F32),
        v((LANES, LANES), BF16),
        v((DEPTHS, LANES, LANES), BF16),
        v((PLANE, LANES, LANES), BF16),
        v((PLANE, LANES, LANES), BF16),
        v((ROWS, LANES), F32),
        v((ROWS, LANES), F32),
        v((8, ROWS), F32),
        v((PEERS, 8, ROWS), F32),
        v((PEERS, 8, LANES), F32),
        v((8, ROWS + LANES), F32),
        v((8, LANES), F32),
        v((16, ROWS), F32),
        v((1, LANES), F32),
        v((DEPTHS * PLANE, 1, LANES), F32),
        dma((13,)),
        dma((2, TILES)),
        dma((4,)),
        dma((7,)),
        dma((7,)),
        dma((DEPTHS,)),
        dma((DEPTHS,)),
        dma((PLANE,)),
    ]


def per_device(
    states,
    inner_weight,
    gate_weight,
    state_weight,
    step_weight,
    step_bias,
    decay_rate,
    skip_gain,
    conv_inner,
    conv_state,
    norm_gain,
    value_weight,
    rewards,
    done_flags,
    horizon,
):
    hbm = pl.BlockSpec(memory_space=pl.ANY)
    vmem = pl.BlockSpec(memory_space=pltpu.VMEM)
    seq_total = states.shape[0] * DEPTHS * PLANE
    results = (
        jax.ShapeDtypeStruct((1, ROWS), F32),
        jax.ShapeDtypeStruct((1, ROWS), F32),
        jax.ShapeDtypeStruct((1, 1), F32),
    )
    packed = pl.pallas_call(
        functools.partial(kernel, seq_total),
        out_shape=jax.ShapeDtypeStruct((3, ROWS), F32),
        in_specs=[hbm] * 15,
        out_specs=vmem,
        scratch_shapes=scratch(),
        compiler_params=pltpu.CompilerParams(
            collective_id=0, has_side_effects=True, vmem_limit_bytes=56 * 2**20
        ),
    )(
        states,
        inner_weight,
        gate_weight,
        state_weight,
        step_weight.T,
        step_bias,
        decay_rate,
        skip_gain,
        conv_inner,
        conv_state,
        norm_gain.reshape(1, -1),
        value_weight.reshape(1, -1),
        rewards.reshape(1, -1),
        done_flags.reshape(1, -1),
        horizon.reshape(1, -1),
    )
    values, targets, loss = pl.pallas_call(
        unpack,
        out_shape=results,
        in_specs=[vmem],
        out_specs=(vmem, vmem, vmem),
    )(packed)
    return values.reshape(-1), targets.reshape(-1), loss.reshape(())


def solution(mesh):
    torus = Mesh(
        mesh.devices.reshape(DEPTHS, 4, 2, mesh.shape["head"]), SEQ + ("head",)
    )
    placed = (
        P(SEQ, None),
        P(None, "head"),
        P(None, "head"),
        P(),
        P(None, "head"),
        P("head"),
        P("head"),
        P("head"),
        P(None, "head"),
        P(),
        P("head"),
        P("head"),
        P(SEQ),
        P(SEQ),
        P(SEQ),
    )
    return jax.shard_map(
        per_device, mesh=torus, in_specs=placed, out_specs=(P(SEQ), P(SEQ), P()), check_vma=False
    )
```

```python
import functools

import jax
import jax.numpy as jnp
from jax import lax
from jax.experimental import pallas as pl
from jax.experimental.pallas import tpu as pltpu
from jax.sharding import Mesh
from jax.sharding import PartitionSpec as P

SEQ = ("seq_0", "seq_1", "seq_2")
MESH = pl.DeviceIdType.MESH
F32 = jnp.float32
BF16 = jnp.bfloat16

KCONV = 4
NSTEP = 8
DISCOUNT = 0.99
EXPECTILE = 0.7
EPSILON = 1e-05

HALO = 16
ROWS = 512
SPANS = ((0, 128), (128, 384))
LONGEST = 384
SOONER = 3
DEPTH = 2048
HEADS = 8
LANES = 128
WIDE = 256
TILE = 512
TILES = HEADS * LANES // TILE
TILE_HEADS = TILE // LANES
PLANE = 8
DEPTHS = 8
PEERS = 4


def silu(value):
    half = 0.5 * value
    return half + half * jnp.tanh(half)


def dot(a, b):
    return jnp.dot(a, b, preferred_element_type=F32)


def three_pieces(value):
    high = value.astype(BF16).astype(F32)
    rest = value - high
    middle = rest.astype(BF16).astype(F32)
    return high, middle, rest - middle


def down(row, rows=LANES):
    return jnp.broadcast_to(row, (rows, row.shape[1])).T


def kernel(
    seq_total,
    states,
    w_in,
    w_gate,
    w_state,
    w_step,
    bias_in,
    rate_in,
    skip_in,
    taps_in,
    taps_st,
    gain,
    weight,
    rewards,
    done,
    horizon,
    out,
    xs,
    wi,
    wg,
    ws,
    wt_in,
    bias,
    rate,
    skip,
    wt,
    tin,
    tst,
    gn,
    vw,
    rw,
    dn,
    hz,
    pre0,
    pre1,
    xh,
    ro,
    rdm,
    wtf,
    sc,
    lrow,
    dtrow,
    drow,
    tail,
    decb,
    recve1,
    dall,
    recve2,
    y,
    gs,
    send1,
    recv1,
    inside,
    reach_in,
    send2,
    recv2,
    send4,
    recv4,
    squares,
    valued_sum,
    part,
    recvh,
    recvn,
    ext,
    recvr,
    coef,
    loss1,
    recvl,
    local_sem,
    tile_sem,
    near_sem,
    send_sem,
    recv_sem,
    s2,
    r2,
    r4,
):
    z, x, c, head = (lax.axis_index(name) for name in SEQ + ("head",))
    here = x * 2 + c
    place = z * PLANE + here
    total = DEPTHS * PLANE
    after = lax.rem(place + 1, total)
    before = lax.rem(place + total - 1, total)

    def of_place(at, at_head):
        return (lax.div(at, PLANE), lax.div(lax.rem(at, PLANE), 2), lax.rem(at, 2), at_head)

    def in_plane(q):
        return (z, lax.div(q, 2), lax.rem(q, 2), head)

    def in_depth(k):
        return (k, x, c, head)

    def in_head(k):
        return (z, x, c, k)

    def put(src, dst, ssem, rsem, device):
        return pltpu.make_async_remote_copy(
            src_ref=src, dst_ref=dst, send_sem=ssem, recv_sem=rsem, device_id=device, device_id_type=MESH
        )

    def others(me, count, act):
        def one(i, carry):
            act(lax.rem(me + i, count))
            return carry

        lax.fori_loop(1, count, one, 0)

    def all_of(ref, count, which):
        whole = ref.at[pl.ds(0, count)]
        return put(whole, whole, send_sem.at[which], recv_sem.at[which], in_head(lax.rem(head + 1, PEERS)))

    small = [
        (states, xs.at[pl.ds(HALO, ROWS), :]),
        (w_step, wt_in),
        (bias_in, bias),
        (rate_in, rate),
        (skip_in, skip),
        (done, dn),
        (rewards, rw),
        (w_state, ws),
        (taps_st, tst),
        (taps_in, tin),
        (gain, gn),
        (weight, vw),
        (horizon, hz),
    ]
    local = [pltpu.make_async_copy(src, dst, local_sem.at[i]) for i, (src, dst) in enumerate(small)]

    def tile_copy(src, dst, slot, which):
        columns = pl.ds(pl.multiple_of(which * TILE, TILE), TILE)
        return pltpu.make_async_copy(src.at[:, columns], dst.at[which], tile_sem.at[slot, which])

    def turned(j):
        return lax.rem(j + x, TILES)

    for i in (0, 1, 5, 6, 2, 3, 4, 8, 9, 7):
        local[i].start()

    barrier = pltpu.get_barrier_semaphore()

    def greet(device):
        pl.semaphore_signal(barrier, inc=1, device_id=device, device_id_type=MESH)

    others(z, DEPTHS, lambda k: greet(in_depth(k)))
    tile_copy(w_in, wi, 0, turned(0)).start()
    greet(of_place(before, head))
    for k in range(PEERS):
        greet(of_place(after, k))
    others(here, PLANE, lambda q: greet(in_plane(q)))
    others(head, PEERS, lambda k: greet(in_head(k)))
    tile_copy(w_in, wi, 0, turned(1)).start()

    local[5].wait()
    local[6].wait()
    alive = 1.0 - dn[...].astype(F32)
    ext[...] = jnp.zeros((8, ROWS + LANES), F32)
    ext[0:1, 0:ROWS] = rw[...]
    ext[1:2, 0:ROWS] = alive
    local[1].wait()
    wt[...] = jnp.concatenate(
        [wt_in[...].astype(F32), jnp.zeros((LANES - HEADS, DEPTH), F32)], axis=0
    ).astype(BF16)
    local[0].wait()
    pl.semaphore_wait(barrier, (PLANE - 1) + (DEPTHS - 1) + (PEERS - 1) + 1 + PEERS)

    halo = put(
        states.at[pl.ds(ROWS - HALO, HALO), :],
        xs.at[pl.ds(0, HALO), :],
        near_sem.at[0],
        near_sem.at[1],
        of_place(after, head),
    )
    halo.start()
    rim = put(
        ext.at[:, pl.ds(0, LANES)], recvr, near_sem.at[2], near_sem.at[3], of_place(before, head)
    )
    rim.start()

    step_pre = lax.dot_general(
        xs[HALO : HALO + ROWS, :],
        wt[...],
        (((1,), (1,)), ((), ())),
        preferred_element_type=F32,
    ).T[0:HEADS, :]
    for i in (2, 3, 4):
        local[i].wait()
    order = lax.broadcasted_iota(jnp.int32, (HEADS, ROWS), 0)
    bias_rows = jnp.zeros((HEADS, ROWS), F32)
    rate_rows = jnp.zeros((HEADS, ROWS), F32)
    for h in range(HEADS):
        bias_rows = jnp.where(order == h, bias[h], bias_rows)
        rate_rows = jnp.where(order == h, rate[h], rate_rows)
    step_pre = step_pre + bias_rows
    step = jnp.maximum(step_pre, 0.0) + jnp.log1p(jnp.exp(-jnp.abs(step_pre)))
    dtrow[...] = step
    done_rows = jnp.broadcast_to(dn[...].astype(F32), (HEADS, ROWS))
    blocks = ROWS // LANES
    pieces = three_pieces(-(rate_rows * step)) + (done_rows,)
    stacked = jnp.concatenate(
        [p[:, b * LANES : (b + 1) * LANES] for p in pieces for b in range(blocks)], axis=0
    ).astype(BF16)
    triangle = (
        lax.broadcasted_iota(jnp.int32, (LANES, LANES), 0)
        <= lax.broadcasted_iota(jnp.int32, (LANES, LANES), 1)
    ).astype(F32).astype(BF16)
    sums = dot(stacked, triangle)
    span = HEADS * blocks
    decays = sums[0:span] + sums[span : 2 * span] + sums[2 * span : 3 * span]
    dones = sums[3 * span : 4 * span]

    def joined(parts):
        found, offset = [], jnp.zeros((HEADS, 1), F32)
        for b in range(blocks):
            block = parts[b * HEADS : (b + 1) * HEADS, :] + offset
            offset = block[:, LANES - 1 : LANES]
            found.append(block)
        return jnp.concatenate(found, axis=1), offset

    running, last = joined(decays)
    done_to, done_all = joined(dones)
    done_before = done_to - done_rows
    lrow[...] = running
    drow[...] = done_before
    tail[...] = jnp.where(done_before == done_all, jnp.exp(last - running) * step, 0.0)
    lost = jnp.broadcast_to(jnp.where(done_all == 0.0, jnp.exp(last), 0.0), (HEADS, LANES))
    decb[...] = lost
    others(
        here,
        PLANE,
        lambda q: put(decb, recve1.at[here], send_sem.at[0], recv_sem.at[0], in_plane(q)).start(),
    )
    recve1[here] = lost

    def convolved(pre, count, taps, columns):
        whole = pre[HALO : HALO + count, columns] * taps[KCONV - 1 : KCONV, :]
        for k in range(KCONV - 1):
            lag = KCONV - 1 - k
            whole = whole + pre[HALO - lag : HALO - lag + count, columns] * taps[k : k + 1, :]
        return silu(whole)

    def project(pre, part_of, tile):
        first, count = SPANS[part_of]
        rows = xs[first : first + HALO + count, :]
        if tile is None:
            pre[0 : HALO + count, 0:WIDE] = dot(rows, ws[...])
        else:
            pre[0 : HALO + count, :] = dot(rows, wi[tile])

    def finish(pre, part_of, tile):
        first, count = SPANS[part_of]
        rows = slice(first, first + count)
        if tile is None:
            wtf[:, rows] = convolved(pre, count, tst[:, 0:LANES], slice(0, LANES)).T
            ro[rows, :] = convolved(pre, count, tst[:, LANES:WIDE], slice(LANES, WIDE))
            return
        for k in range(TILE_HEADS):
            h = tile * TILE_HEADS + k
            taps = tin[:, pl.ds(pl.multiple_of(h * LANES, LANES), LANES)]
            conv = convolved(pre, count, taps, slice(k * LANES, (k + 1) * LANES))
            xh[h, rows, :] = conv.astype(BF16)

    def gained(tile):
        for k in range(TILE_HEADS):
            h = tile * TILE_HEADS + k
            added = dot((wtf[...] * tail[pl.ds(h, 1), :]).astype(BF16), xh[h])
            send1[h] = added.astype(BF16)

    def send_gained(tile):
        for k in range(TILE_HEADS):
            h = tile * TILE_HEADS + k

            @pl.when(h != here)
            def _():
                put(
                    send1.at[h], recv1.at[here], send_sem.at[1], recv_sem.at[1], in_plane(h)
                ).start()

    def gate_tile(j):
        tile_copy(w_gate, wg, 1, j).wait()
        gate = silu(dot(xs[HALO : HALO + ROWS, :], wg[j]))
        for k in range(TILE_HEADS):
            gs[j * TILE_HEADS + k] = gate[:, k * LANES : (k + 1) * LANES]

    pres = (pre0, pre1)
    tiles = [None] + [turned(j) for j in range(TILES)]

    for i in (7, 8, 9):
        local[i].wait()
    project(pres[0], 1, None)
    for i in range(1, TILES + 1):
        tile_copy(w_in, wi, 0, tiles[i]).wait()
        project(pres[i % 2], 1, tiles[i])
        finish(pres[(i - 1) % 2], 1, tiles[i - 1])
    for j in range(TILES):
        tile_copy(w_gate, wg, 1, j).start()
    for i in (10, 11, 12):
        local[i].start()
    finish(pres[TILES % 2], 1, tiles[TILES])

    halo.wait_recv()
    xs[0:HALO, :] = jnp.where(place > 0, xs[0:HALO, :].astype(F32), 0.0).astype(BF16)
    project(pres[0], 0, None)
    for i in range(1, TILES + 1):
        project(pres[i % 2], 0, tiles[i])
        finish(pres[(i - 1) % 2], 0, tiles[i - 1])
        if i > 1:
            gained(tiles[i - 1])
            send_gained(tiles[i - 1])
    finish(pres[TILES % 2], 0, tiles[TILES])
    gained(tiles[TILES])
    send_gained(tiles[TILES])

    all_of(recve1, PLANE - 1, 0).wait_recv()
    plane_lost = recve1[0]
    for q in range(1, PLANE):
        plane_lost = plane_lost * recve1[q]
    dall[...] = plane_lost
    others(
        z,
        DEPTHS,
        lambda k: put(dall, recve2.at[z], send_sem.at[2], recv_sem.at[2], in_depth(k)).start(),
    )
    recve2[z] = plane_lost
    recv1[here] = send1[here]

    for j in range(TILES):
        gate_tile(j)

    all_of(recv1, PLANE - 1, 1).wait_recv()

    def plane_step(q, carry):
        state, lasting = carry
        inside[q] = state
        reach_in[q] = jnp.broadcast_to(lasting, (8, LANES))
        lost = recve1[q, pl.ds(here, 1), :]
        return lost * state + recv1[q].astype(F32), lasting * lost

    state, _ = lax.fori_loop(
        0, PLANE, plane_step, (jnp.zeros((LANES, LANES), F32), jnp.ones((1, LANES), F32))
    )
    send2[...] = state.astype(BF16)

    def to_later(k):
        return put(send2, recv2.at[z], s2.at[k], r2.at[z], in_depth(k))

    def later(act):
        def one(k, carry):
            act(k)
            return carry

        lax.fori_loop(z + 1, DEPTHS, one, 0)

    later(lambda k: to_later(k).start())

    done_row = drow[0:1, :]
    done_down = down(done_row)
    rdm[...] = jnp.where(done_down == 0.0, ro[...], 0.0).astype(BF16)
    readout = ro[...].astype(BF16)
    writes_t = wtf[...].astype(BF16)
    for b in range(2):
        rows = slice(b * WIDE, (b + 1) * WIDE)
        upto = (b + 1) * WIDE
        scores = dot(readout[rows, :], writes_t[:, 0:upto])
        at_row = lax.broadcasted_iota(jnp.int32, (WIDE, LANES), 0) + b * WIDE
        for k in range(upto // LANES):
            columns = slice(k * LANES, (k + 1) * LANES)
            at_column = lax.broadcasted_iota(jnp.int32, (WIDE, LANES), 1) + k * LANES
            seen = (at_row >= at_column) & (done_down[rows, :] == done_row[:, columns])
            sc[rows, columns] = jnp.where(seen, scores[:, columns], 0.0)

    def own_scan(h, carry):
        across = lrow[pl.ds(h, 1), :]
        step_across = dtrow[pl.ds(h, 1), :]
        along = down(across)
        inner = xh[h]
        for b in range(2):
            rows = slice(b * WIDE, (b + 1) * WIDE)
            upto = (b + 1) * WIDE
            weights = []
            for k in range(upto // LANES):
                columns = slice(k * LANES, (k + 1) * LANES)
                gap = jnp.minimum(along[rows, :] - across[:, columns], 0.0)
                weights.append((jnp.exp(gap) * step_across[:, columns] * sc[rows, columns]).astype(BF16))
            mixed = dot(jnp.concatenate(weights, axis=1), inner[0:upto, :])
            y[h, rows, :] = (mixed + skip[h] * inner[rows, :].astype(F32)) * gs[h, rows, :]
        gs[h] = jnp.exp(along) * gs[h]
        return carry

    lax.fori_loop(0, SOONER, own_scan, 0)

    all_of(recve2, DEPTHS - 1, 2).wait_recv()

    def depth_step(k, state):
        put(send2, recv2.at[k], s2.at[k], r2.at[k], in_depth(k)).wait_recv()
        return recve2[k, pl.ds(here, 1), :] * state + recv2[k].astype(F32)

    entering = lax.fori_loop(0, z, depth_step, jnp.zeros((LANES, LANES), F32))

    def carried(q):
        send4[q] = (reach_in[q][0:1, :] * entering + inside[q]).astype(BF16)

    def hand_out(q):
        carried(q)
        put(send4.at[q], recv4.at[here], send_sem.at[3], r4.at[here], in_plane(q)).start()

    others(here, PLANE, hand_out)
    carried(here)
    recv4[here] = send4[here]

    lax.fori_loop(SOONER, HEADS, own_scan, 0)

    for i in (10, 11, 12):
        local[i].wait()
    rim.wait_recv()
    is_last = place == total - 1
    ext[:, ROWS : ROWS + LANES] = jnp.where(is_last, 0.0, recvr[...])
    length = ROWS + LANES
    survive = jnp.ones((1, ROWS), F32)
    rewarded = jnp.zeros((1, ROWS), F32)
    for k in range(NSTEP + 1):
        ahead = ext[...] if k == 0 else pltpu.roll(ext[...], length - k, 1)
        factor = DISCOUNT**k * survive
        rewarded = rewarded + jnp.where(k < hz[...], factor * ahead[0:1, 0:ROWS], 0.0)
        coef[k : k + 1, :] = jnp.where(k == hz[...], factor, 0.0)
        survive = survive * ahead[1:2, 0:ROWS]
    coef[NSTEP + 1 : NSTEP + 2, :] = rewarded
    gn[...] = gn[...] * vw[...]

    def mix(h):
        gated = y[h] + dot(rdm[...], recv4[h]) * gs[h]
        scale = gn[:, pl.ds(pl.multiple_of(h * LANES, LANES), LANES)]
        return gated * gated, gated * scale

    squares[...], valued_sum[...] = mix(here)

    def mix_arrived(i, carry):
        h = lax.rem(here + PLANE - i, PLANE)
        put(send4.at[h], recv4.at[h], send_sem.at[3], r4.at[h], in_plane(h)).wait_recv()
        more_squares, more_valued = mix(h)
        squares[...] = squares[...] + more_squares
        valued_sum[...] = valued_sum[...] + more_valued
        return carry

    lax.fori_loop(1, PLANE, mix_arrived, 0)

    def to_before(k):
        return put(
            part.at[:, pl.ds(0, LANES)],
            recvn.at[head],
            send_sem.at[5],
            recv_sem.at[5],
            of_place(before, k),
        )

    for first, past in ((0, LANES), (LANES, ROWS)):
        part[0:1, first:past] = jnp.sum(squares[first:past, :].T, axis=0, keepdims=True)
        part[1:2, first:past] = jnp.sum(valued_sum[first:past, :].T, axis=0, keepdims=True)
        if first == 0:
            for k in range(PEERS):
                to_before(k).start()
    others(
        head,
        PEERS,
        lambda k: put(part, recvh.at[head], send_sem.at[4], recv_sem.at[4], in_head(k)).start(),
    )
    recvh[head] = part[...]
    all_of(recvh, PEERS - 1, 4).wait_recv()
    all_of(recvn, PEERS, 5).wait_recv()

    def normed(sums):
        return sums[1:2, :] * lax.rsqrt(sums[0:1, :] / (PEERS * HEADS * LANES) + EPSILON)

    own = normed(recvh[0] + recvh[1] + recvh[2] + recvh[3])
    following = normed(recvn[0] + recvn[1] + recvn[2] + recvn[3])
    following = jnp.where(is_last, 0.0, following)
    valued = jnp.broadcast_to(jnp.concatenate([own, following], axis=1), (8, length))
    targets = coef[NSTEP + 1 : NSTEP + 2, :]
    for k in range(NSTEP + 1):
        ahead = valued if k == 0 else pltpu.roll(valued, length - k, 1)
        targets = targets + coef[k : k + 1, :] * ahead[0:1, 0:ROWS]
    residual = targets - own
    terms = jnp.where(residual < 0, 1.0 - EXPECTILE, EXPECTILE) * residual * residual
    mine = jnp.broadcast_to(jnp.sum(terms, axis=1, keepdims=True), (1, LANES))
    loss1[...] = mine

    def tell(device):
        put(loss1, recvl.at[place], send_sem.at[6], recv_sem.at[6], device).start()

    def tell_plane(k):
        for q in range(PLANE):
            tell((k, q // 2, q % 2, head))

    def tell_planes(first, past):
        def one(k, carry):
            tell_plane(k)
            return carry

        lax.fori_loop(first, past, one, 0)

    tell_planes(0, z)
    tell_planes(z + 1, DEPTHS)
    others(here, PLANE, lambda q: tell(in_plane(q)))
    recvl[place] = mine
    out[0:1, :] = own
    out[1:2, :] = targets

    halo.wait_send()
    rim.wait_send()
    all_of(recve1, PLANE - 1, 0).wait_send()
    all_of(recv1, PLANE - 1, 1).wait_send()
    all_of(recve2, DEPTHS - 1, 2).wait_send()
    all_of(recv4, PLANE - 1, 3).wait_send()
    all_of(recvh, PEERS - 1, 4).wait_send()
    all_of(recvn, PEERS, 5).wait_send()
    later(lambda k: to_later(k).wait_send())

    all_of(recvl, total - 1, 6).wait_recv()
    out[2:3, 0:LANES] = jnp.sum(recvl[...], axis=0) / seq_total
    all_of(recvl, total - 1, 6).wait_send()


def unpack(packed, values, targets, loss):
    values[...] = packed[0:1, :]
    targets[...] = packed[1:2, :]
    loss[...] = packed[2:3, 0:1]


def scratch():
    v = pltpu.VMEM
    dma = pltpu.SemaphoreType.DMA
    return [
        v((HALO + ROWS, DEPTH), BF16),
        v((TILES, DEPTH, TILE), BF16),
        v((TILES, DEPTH, TILE), BF16),
        v((DEPTH, WIDE), BF16),
        v((HEADS, DEPTH), BF16),
        pltpu.SMEM((HEADS,), F32),
        pltpu.SMEM((HEADS,), F32),
        pltpu.SMEM((HEADS,), F32),
        v((LANES, DEPTH), BF16),
        v((KCONV, HEADS * LANES), F32),
        v((KCONV, WIDE), F32),
        v((1, HEADS * LANES), F32),
        v((1, HEADS * LANES), F32),
        v((1, ROWS), F32),
        v((1, ROWS), jnp.int32),
        v((1, ROWS), jnp.int32),
        v((HALO + LONGEST, TILE), F32),
        v((HALO + LONGEST, TILE), F32),
        v((HEADS, ROWS, LANES), BF16),
        v((ROWS, LANES), F32),
        v((ROWS, LANES), BF16),
        v((LANES, ROWS), F32),
        v((ROWS, ROWS), F32),
        v((HEADS, ROWS), F32),
        v((HEADS, ROWS), F32),
        v((HEADS, ROWS), F32),
        v((HEADS, ROWS), F32),
        v((HEADS, LANES), F32),
        v((PLANE, HEADS, LANES), F32),
        v((HEADS, LANES), F32),
        v((DEPTHS, HEADS, LANES), F32),
        v((HEADS, ROWS, LANES), F32),
        v((HEADS, ROWS, LANES), F32),
        v((PLANE, LANES, LANES), BF16),
        v((PLANE, LANES, LANES), BF16),
        v((PLANE, LANES, LANES), F32),
        v((PLANE, 8, LANES), F32),
        v((LANES, LANES), BF16),
        v((DEPTHS, LANES, LANES), BF16),
        v((PLANE, LANES, LANES), BF16),
        v((PLANE, LANES, LANES), BF16),
        v((ROWS, LANES), F32),
        v((ROWS, LANES), F32),
        v((2, ROWS), F32),
        v((PEERS, 2, ROWS), F32),
        v((PEERS, 2, LANES), F32),
        v((8, ROWS + LANES), F32),
        v((8, LANES), F32),
        v((16, ROWS), F32),
        v((1, LANES), F32),
        v((DEPTHS * PLANE, 1, LANES), F32),
        dma((13,)),
        dma((2, TILES)),
        dma((4,)),
        dma((7,)),
        dma((7,)),
        dma((DEPTHS,)),
        dma((DEPTHS,)),
        dma((PLANE,)),
    ]


def per_device(
    states,
    inner_weight,
    gate_weight,
    state_weight,
    step_weight,
    step_bias,
    decay_rate,
    skip_gain,
    conv_inner,
    conv_state,
    norm_gain,
    value_weight,
    rewards,
    done_flags,
    horizon,
):
    hbm = pl.BlockSpec(memory_space=pl.ANY)
    vmem = pl.BlockSpec(memory_space=pltpu.VMEM)
    seq_total = states.shape[0] * DEPTHS * PLANE
    results = (
        jax.ShapeDtypeStruct((1, ROWS), F32),
        jax.ShapeDtypeStruct((1, ROWS), F32),
        jax.ShapeDtypeStruct((1, 1), F32),
    )
    packed = pl.pallas_call(
        functools.partial(kernel, seq_total),
        out_shape=jax.ShapeDtypeStruct((3, ROWS), F32),
        in_specs=[hbm] * 15,
        out_specs=vmem,
        scratch_shapes=scratch(),
        compiler_params=pltpu.CompilerParams(
            collective_id=0, has_side_effects=True, vmem_limit_bytes=56 * 2**20
        ),
    )(
        states,
        inner_weight,
        gate_weight,
        state_weight,
        step_weight.T,
        step_bias,
        decay_rate,
        skip_gain,
        conv_inner,
        conv_state,
        norm_gain.reshape(1, -1),
        value_weight.reshape(1, -1),
        rewards.reshape(1, -1),
        done_flags.reshape(1, -1),
        horizon.reshape(1, -1),
    )
    values, targets, loss = pl.pallas_call(
        unpack,
        out_shape=results,
        in_specs=[vmem],
        out_specs=(vmem, vmem, vmem),
    )(packed)
    return values.reshape(-1), targets.reshape(-1), loss.reshape(())


def solution(mesh):
    torus = Mesh(
        mesh.devices.reshape(DEPTHS, 4, 2, mesh.shape["head"]), SEQ + ("head",)
    )
    placed = (
        P(SEQ, None),
        P(None, "head"),
        P(None, "head"),
        P(),
        P(None, "head"),
        P("head"),
        P("head"),
        P("head"),
        P(None, "head"),
        P(),
        P("head"),
        P("head"),
        P(SEQ),
        P(SEQ),
        P(SEQ),
    )
    return jax.shard_map(
        per_device, mesh=torus, in_specs=placed, out_specs=(P(SEQ), P(SEQ), P()), check_vma=False
    )
```

```python
import functools

import jax
import jax.numpy as jnp
from jax import lax
from jax.experimental import pallas as pl
from jax.experimental.pallas import tpu as pltpu
from jax.sharding import Mesh
from jax.sharding import PartitionSpec as P

SEQ = ("seq_0", "seq_1", "seq_2")
MESH = pl.DeviceIdType.MESH
F32 = jnp.float32
BF16 = jnp.bfloat16

KCONV = 4
NSTEP = 8
DISCOUNT = 0.99
EXPECTILE = 0.7
EPSILON = 1e-05

HALO = 16
ROWS = 512
SPANS = ((0, 128), (128, 384))
LONGEST = 384
SOONER = 3
DEPTH = 2048
HEADS = 8
LANES = 128
WIDE = 256
TILE = 512
TILES = HEADS * LANES // TILE
TILE_HEADS = TILE // LANES
PLANE = 8
DEPTHS = 8
PEERS = 4


def silu(value):
    half = 0.5 * value
    return half + half * jnp.tanh(half)


def dot(a, b):
    return jnp.dot(a, b, preferred_element_type=F32)


def three_pieces(value):
    high = value.astype(BF16).astype(F32)
    rest = value - high
    middle = rest.astype(BF16).astype(F32)
    return high, middle, rest - middle


def down(row, rows=LANES):
    return jnp.broadcast_to(row, (rows, row.shape[1])).T


def kernel(
    seq_total,
    states,
    w_in,
    w_gate,
    w_state,
    w_step,
    bias_in,
    rate_in,
    skip_in,
    taps_in,
    taps_st,
    gain,
    weight,
    rewards,
    done,
    horizon,
    out,
    xs,
    wi,
    wg,
    ws,
    wt_in,
    bias,
    rate,
    skip,
    wt,
    tin,
    tst,
    gn,
    vw,
    rw,
    dn,
    hz,
    pre0,
    pre1,
    xh,
    ro,
    rdm,
    wtf,
    sc,
    lrow,
    dtrow,
    drow,
    tail,
    decb,
    recve1,
    dall,
    recve2,
    y,
    gs,
    send1,
    recv1,
    inside,
    reach_in,
    send2,
    recv2,
    send4,
    recv4,
    squares,
    valued_sum,
    part,
    recvh,
    recvn,
    ext,
    recvr,
    coef,
    loss1,
    recvl,
    local_sem,
    tile_sem,
    near_sem,
    send_sem,
    recv_sem,
    s2,
    r2,
    r4,
):
    z, x, c, head = (lax.axis_index(name) for name in SEQ + ("head",))
    here = x * 2 + c
    place = z * PLANE + here
    total = DEPTHS * PLANE
    after = lax.rem(place + 1, total)
    before = lax.rem(place + total - 1, total)

    def of_place(at, at_head):
        return (lax.div(at, PLANE), lax.div(lax.rem(at, PLANE), 2), lax.rem(at, 2), at_head)

    def in_plane(q):
        return (z, lax.div(q, 2), lax.rem(q, 2), head)

    def in_depth(k):
        return (k, x, c, head)

    def in_head(k):
        return (z, x, c, k)

    def put(src, dst, ssem, rsem, device):
        return pltpu.make_async_remote_copy(
            src_ref=src, dst_ref=dst, send_sem=ssem, recv_sem=rsem, device_id=device, device_id_type=MESH
        )

    def others(me, count, act):
        def one(i, carry):
            act(lax.rem(me + i, count))
            return carry

        lax.fori_loop(1, count, one, 0)

    def all_of(ref, count, which):
        whole = ref.at[pl.ds(0, count)]
        return put(whole, whole, send_sem.at[which], recv_sem.at[which], in_head(lax.rem(head + 1, PEERS)))

    small = [
        (states, xs.at[pl.ds(HALO, ROWS), :]),
        (w_step, wt_in),
        (bias_in, bias),
        (rate_in, rate),
        (skip_in, skip),
        (done, dn),
        (rewards, rw),
        (w_state, ws),
        (taps_st, tst),
        (taps_in, tin),
        (gain, gn),
        (weight, vw),
        (horizon, hz),
    ]
    local = [pltpu.make_async_copy(src, dst, local_sem.at[i]) for i, (src, dst) in enumerate(small)]

    def tile_copy(src, dst, slot, which):
        columns = pl.ds(pl.multiple_of(which * TILE, TILE), TILE)
        return pltpu.make_async_copy(src.at[:, columns], dst.at[which], tile_sem.at[slot, which])

    def turned(j):
        return lax.rem(j + x, TILES)

    for i in (0, 1, 5, 6, 2, 3, 4, 8, 9, 7):
        local[i].start()

    barrier = pltpu.get_barrier_semaphore()

    def greet(device):
        pl.semaphore_signal(barrier, inc=1, device_id=device, device_id_type=MESH)

    others(z, DEPTHS, lambda k: greet(in_depth(k)))
    tile_copy(w_in, wi, 0, turned(0)).start()
    greet(of_place(before, head))
    for k in range(PEERS):
        greet(of_place(after, k))
    others(here, PLANE, lambda q: greet(in_plane(q)))
    others(head, PEERS, lambda k: greet(in_head(k)))
    tile_copy(w_in, wi, 0, turned(1)).start()

    local[5].wait()
    local[6].wait()
    alive = 1.0 - dn[...].astype(F32)
    ext[...] = jnp.zeros((8, ROWS + LANES), F32)
    ext[0:1, 0:ROWS] = rw[...]
    ext[1:2, 0:ROWS] = alive
    local[1].wait()
    wt[...] = jnp.concatenate(
        [wt_in[...].astype(F32), jnp.zeros((LANES - HEADS, DEPTH), F32)], axis=0
    ).astype(BF16)
    local[0].wait()

    step_pre = lax.dot_general(
        xs[HALO : HALO + ROWS, :],
        wt[...],
        (((1,), (1,)), ((), ())),
        preferred_element_type=F32,
    ).T[0:HEADS, :]
    for i in (2, 3, 4):
        local[i].wait()
    order = lax.broadcasted_iota(jnp.int32, (HEADS, ROWS), 0)
    bias_rows = jnp.zeros((HEADS, ROWS), F32)
    rate_rows = jnp.zeros((HEADS, ROWS), F32)
    for h in range(HEADS):
        bias_rows = jnp.where(order == h, bias[h], bias_rows)
        rate_rows = jnp.where(order == h, rate[h], rate_rows)
    step_pre = step_pre + bias_rows
    step = jnp.maximum(step_pre, 0.0) + jnp.log1p(jnp.exp(-jnp.abs(step_pre)))
    dtrow[...] = step
    done_rows = jnp.broadcast_to(dn[...].astype(F32), (HEADS, ROWS))
    blocks = ROWS // LANES
    pieces = three_pieces(-(rate_rows * step)) + (done_rows,)
    stacked = jnp.concatenate(
        [p[:, b * LANES : (b + 1) * LANES] for p in pieces for b in range(blocks)], axis=0
    ).astype(BF16)
    triangle = (
        lax.broadcasted_iota(jnp.int32, (LANES, LANES), 0)
        <= lax.broadcasted_iota(jnp.int32, (LANES, LANES), 1)
    ).astype(F32).astype(BF16)
    sums = dot(stacked, triangle)
    span = HEADS * blocks
    decays = sums[0:span] + sums[span : 2 * span] + sums[2 * span : 3 * span]
    dones = sums[3 * span : 4 * span]

    def joined(parts):
        found, offset = [], jnp.zeros((HEADS, 1), F32)
        for b in range(blocks):
            block = parts[b * HEADS : (b + 1) * HEADS, :] + offset
            offset = block[:, LANES - 1 : LANES]
            found.append(block)
        return jnp.concatenate(found, axis=1), offset

    running, last = joined(decays)
    done_to, done_all = joined(dones)
    done_before = done_to - done_rows
    lrow[...] = running
    drow[...] = done_before
    tail[...] = jnp.where(done_before == done_all, jnp.exp(last - running) * step, 0.0)
    lost = jnp.broadcast_to(jnp.where(done_all == 0.0, jnp.exp(last), 0.0), (HEADS, LANES))
    decb[...] = lost

    pl.semaphore_wait(barrier, (PLANE - 1) + (DEPTHS - 1) + (PEERS - 1) + 1 + PEERS)

    halo = put(
        states.at[pl.ds(ROWS - HALO, HALO), :],
        xs.at[pl.ds(0, HALO), :],
        near_sem.at[0],
        near_sem.at[1],
        of_place(after, head),
    )
    halo.start()
    rim = put(
        ext.at[:, pl.ds(0, LANES)], recvr, near_sem.at[2], near_sem.at[3], of_place(before, head)
    )
    rim.start()

    others(
        here,
        PLANE,
        lambda q: put(decb, recve1.at[here], send_sem.at[0], recv_sem.at[0], in_plane(q)).start(),
    )
    recve1[here] = lost

    def convolved(pre, count, taps, columns):
        whole = pre[HALO : HALO + count, columns] * taps[KCONV - 1 : KCONV, :]
        for k in range(KCONV - 1):
            lag = KCONV - 1 - k
            whole = whole + pre[HALO - lag : HALO - lag + count, columns] * taps[k : k + 1, :]
        return silu(whole)

    def project(pre, part_of, tile):
        first, count = SPANS[part_of]
        rows = xs[first : first + HALO + count, :]
        if tile is None:
            pre[0 : HALO + count, 0:WIDE] = dot(rows, ws[...])
        else:
            pre[0 : HALO + count, :] = dot(rows, wi[tile])

    def finish(pre, part_of, tile):
        first, count = SPANS[part_of]
        rows = slice(first, first + count)
        if tile is None:
            wtf[:, rows] = convolved(pre, count, tst[:, 0:LANES], slice(0, LANES)).T
            ro[rows, :] = convolved(pre, count, tst[:, LANES:WIDE], slice(LANES, WIDE))
            return
        for k in range(TILE_HEADS):
            h = tile * TILE_HEADS + k
            taps = tin[:, pl.ds(pl.multiple_of(h * LANES, LANES), LANES)]
            conv = convolved(pre, count, taps, slice(k * LANES, (k + 1) * LANES))
            xh[h, rows, :] = conv.astype(BF16)

    def gained(tile):
        for k in range(TILE_HEADS):
            h = tile * TILE_HEADS + k
            added = dot((wtf[...] * tail[pl.ds(h, 1), :]).astype(BF16), xh[h])
            send1[h] = added.astype(BF16)

    def send_gained(tile):
        for k in range(TILE_HEADS):
            h = tile * TILE_HEADS + k

            @pl.when(h != here)
            def _():
                put(
                    send1.at[h], recv1.at[here], send_sem.at[1], recv_sem.at[1], in_plane(h)
                ).start()

    def gate_tile(j):
        tile_copy(w_gate, wg, 1, j).wait()
        gate = silu(dot(xs[HALO : HALO + ROWS, :], wg[j]))
        for k in range(TILE_HEADS):
            gs[j * TILE_HEADS + k] = gate[:, k * LANES : (k + 1) * LANES]

    pres = (pre0, pre1)
    tiles = [None] + [turned(j) for j in range(TILES)]

    for i in (7, 8, 9):
        local[i].wait()
    project(pres[0], 1, None)
    for i in range(1, TILES + 1):
        tile_copy(w_in, wi, 0, tiles[i]).wait()
        project(pres[i % 2], 1, tiles[i])
        finish(pres[(i - 1) % 2], 1, tiles[i - 1])
    for j in range(TILES):
        tile_copy(w_gate, wg, 1, j).start()
    for i in (10, 11, 12):
        local[i].start()
    finish(pres[TILES % 2], 1, tiles[TILES])

    halo.wait_recv()
    xs[0:HALO, :] = jnp.where(place > 0, xs[0:HALO, :].astype(F32), 0.0).astype(BF16)
    project(pres[0], 0, None)
    for i in range(1, TILES + 1):
        project(pres[i % 2], 0, tiles[i])
        finish(pres[(i - 1) % 2], 0, tiles[i - 1])
        if i > 1:
            gained(tiles[i - 1])
            send_gained(tiles[i - 1])
    finish(pres[TILES % 2], 0, tiles[TILES])
    gained(tiles[TILES])
    send_gained(tiles[TILES])

    all_of(recve1, PLANE - 1, 0).wait_recv()
    plane_lost = recve1[0]
    for q in range(1, PLANE):
        plane_lost = plane_lost * recve1[q]
    dall[...] = plane_lost
    others(
        z,
        DEPTHS,
        lambda k: put(dall, recve2.at[z], send_sem.at[2], recv_sem.at[2], in_depth(k)).start(),
    )
    recve2[z] = plane_lost
    recv1[here] = send1[here]

    for j in range(TILES):
        gate_tile(j)

    all_of(recv1, PLANE - 1, 1).wait_recv()

    def plane_step(q, carry):
        state, lasting = carry
        inside[q] = state
        reach_in[q] = jnp.broadcast_to(lasting, (8, LANES))
        lost = recve1[q, pl.ds(here, 1), :]
        return lost * state + recv1[q].astype(F32), lasting * lost

    state, _ = lax.fori_loop(
        0, PLANE, plane_step, (jnp.zeros((LANES, LANES), F32), jnp.ones((1, LANES), F32))
    )
    send2[...] = state.astype(BF16)

    def to_later(k):
        return put(send2, recv2.at[z], s2.at[k], r2.at[z], in_depth(k))

    def later(act):
        def one(k, carry):
            act(k)
            return carry

        lax.fori_loop(z + 1, DEPTHS, one, 0)

    later(lambda k: to_later(k).start())

    done_row = drow[0:1, :]
    done_down = down(done_row)
    rdm[...] = jnp.where(done_down == 0.0, ro[...], 0.0).astype(BF16)
    readout = ro[...].astype(BF16)
    writes_t = wtf[...].astype(BF16)
    for b in range(2):
        rows = slice(b * WIDE, (b + 1) * WIDE)
        upto = (b + 1) * WIDE
        scores = dot(readout[rows, :], writes_t[:, 0:upto])
        at_row = lax.broadcasted_iota(jnp.int32, (WIDE, LANES), 0) + b * WIDE
        for k in range(upto // LANES):
            columns = slice(k * LANES, (k + 1) * LANES)
            at_column = lax.broadcasted_iota(jnp.int32, (WIDE, LANES), 1) + k * LANES
            seen = (at_row >= at_column) & (done_down[rows, :] == done_row[:, columns])
            sc[rows, columns] = jnp.where(seen, scores[:, columns], 0.0)

    def own_scan(h, carry):
        across = lrow[pl.ds(h, 1), :]
        step_across = dtrow[pl.ds(h, 1), :]
        along = down(across)
        inner = xh[h]
        for b in range(2):
            rows = slice(b * WIDE, (b + 1) * WIDE)
            upto = (b + 1) * WIDE
            weights = []
            for k in range(upto // LANES):
                columns = slice(k * LANES, (k + 1) * LANES)
                gap = jnp.minimum(along[rows, :] - across[:, columns], 0.0)
                weights.append((jnp.exp(gap) * step_across[:, columns] * sc[rows, columns]).astype(BF16))
            mixed = dot(jnp.concatenate(weights, axis=1), inner[0:upto, :])
            y[h, rows, :] = (mixed + skip[h] * inner[rows, :].astype(F32)) * gs[h, rows, :]
        gs[h] = jnp.exp(along) * gs[h]
        return carry

    lax.fori_loop(0, SOONER, own_scan, 0)

    all_of(recve2, DEPTHS - 1, 2).wait_recv()

    def depth_step(k, state):
        put(send2, recv2.at[k], s2.at[k], r2.at[k], in_depth(k)).wait_recv()
        return recve2[k, pl.ds(here, 1), :] * state + recv2[k].astype(F32)

    entering = lax.fori_loop(0, z, depth_step, jnp.zeros((LANES, LANES), F32))

    def carried(q):
        send4[q] = (reach_in[q][0:1, :] * entering + inside[q]).astype(BF16)

    def hand_out(q):
        carried(q)
        put(send4.at[q], recv4.at[here], send_sem.at[3], r4.at[here], in_plane(q)).start()

    others(here, PLANE, hand_out)
    carried(here)
    recv4[here] = send4[here]

    lax.fori_loop(SOONER, HEADS, own_scan, 0)

    for i in (10, 11, 12):
        local[i].wait()
    rim.wait_recv()
    is_last = place == total - 1
    ext[:, ROWS : ROWS + LANES] = jnp.where(is_last, 0.0, recvr[...])
    length = ROWS + LANES
    survive = jnp.ones((1, ROWS), F32)
    rewarded = jnp.zeros((1, ROWS), F32)
    for k in range(NSTEP + 1):
        ahead = ext[...] if k == 0 else pltpu.roll(ext[...], length - k, 1)
        factor = DISCOUNT**k * survive
        rewarded = rewarded + jnp.where(k < hz[...], factor * ahead[0:1, 0:ROWS], 0.0)
        coef[k : k + 1, :] = jnp.where(k == hz[...], factor, 0.0)
        survive = survive * ahead[1:2, 0:ROWS]
    coef[NSTEP + 1 : NSTEP + 2, :] = rewarded
    gn[...] = gn[...] * vw[...]

    def mix(h):
        gated = y[h] + dot(rdm[...], recv4[h]) * gs[h]
        scale = gn[:, pl.ds(pl.multiple_of(h * LANES, LANES), LANES)]
        return gated * gated, gated * scale

    squares[...], valued_sum[...] = mix(here)

    def mix_arrived(i, carry):
        h = lax.rem(here + PLANE - i, PLANE)
        put(send4.at[h], recv4.at[h], send_sem.at[3], r4.at[h], in_plane(h)).wait_recv()
        more_squares, more_valued = mix(h)
        squares[...] = squares[...] + more_squares
        valued_sum[...] = valued_sum[...] + more_valued
        return carry

    lax.fori_loop(1, PLANE, mix_arrived, 0)

    def to_before(k):
        return put(
            part.at[:, pl.ds(0, LANES)],
            recvn.at[head],
            send_sem.at[5],
            recv_sem.at[5],
            of_place(before, k),
        )

    for first, past in ((0, LANES), (LANES, ROWS)):
        part[0:1, first:past] = jnp.sum(squares[first:past, :].T, axis=0, keepdims=True)
        part[1:2, first:past] = jnp.sum(valued_sum[first:past, :].T, axis=0, keepdims=True)
        if first == 0:
            for k in range(PEERS):
                to_before(k).start()
    others(
        head,
        PEERS,
        lambda k: put(part, recvh.at[head], send_sem.at[4], recv_sem.at[4], in_head(k)).start(),
    )
    recvh[head] = part[...]
    all_of(recvh, PEERS - 1, 4).wait_recv()
    all_of(recvn, PEERS, 5).wait_recv()

    def normed(sums):
        return sums[1:2, :] * lax.rsqrt(sums[0:1, :] / (PEERS * HEADS * LANES) + EPSILON)

    own = normed(recvh[0] + recvh[1] + recvh[2] + recvh[3])
    following = normed(recvn[0] + recvn[1] + recvn[2] + recvn[3])
    following = jnp.where(is_last, 0.0, following)
    valued = jnp.broadcast_to(jnp.concatenate([own, following], axis=1), (8, length))
    targets = coef[NSTEP + 1 : NSTEP + 2, :]
    for k in range(NSTEP + 1):
        ahead = valued if k == 0 else pltpu.roll(valued, length - k, 1)
        targets = targets + coef[k : k + 1, :] * ahead[0:1, 0:ROWS]
    residual = targets - own
    terms = jnp.where(residual < 0, 1.0 - EXPECTILE, EXPECTILE) * residual * residual
    mine = jnp.broadcast_to(jnp.sum(terms, axis=1, keepdims=True), (1, LANES))
    loss1[...] = mine

    def tell(device):
        put(loss1, recvl.at[place], send_sem.at[6], recv_sem.at[6], device).start()

    def tell_plane(k):
        for q in range(PLANE):
            tell((k, q // 2, q % 2, head))

    def tell_planes(first, past):
        def one(k, carry):
            tell_plane(k)
            return carry

        lax.fori_loop(first, past, one, 0)

    tell_planes(0, z)
    tell_planes(z + 1, DEPTHS)
    others(here, PLANE, lambda q: tell(in_plane(q)))
    recvl[place] = mine
    out[0:1, :] = own
    out[1:2, :] = targets

    halo.wait_send()
    rim.wait_send()
    all_of(recve1, PLANE - 1, 0).wait_send()
    all_of(recv1, PLANE - 1, 1).wait_send()
    all_of(recve2, DEPTHS - 1, 2).wait_send()
    all_of(recv4, PLANE - 1, 3).wait_send()
    all_of(recvh, PEERS - 1, 4).wait_send()
    all_of(recvn, PEERS, 5).wait_send()
    later(lambda k: to_later(k).wait_send())

    all_of(recvl, total - 1, 6).wait_recv()
    out[2:3, 0:LANES] = jnp.sum(recvl[...], axis=0) / seq_total
    all_of(recvl, total - 1, 6).wait_send()


def unpack(packed, values, targets, loss):
    values[...] = packed[0:1, :]
    targets[...] = packed[1:2, :]
    loss[...] = packed[2:3, 0:1]


def scratch():
    v = pltpu.VMEM
    dma = pltpu.SemaphoreType.DMA
    return [
        v((HALO + ROWS, DEPTH), BF16),
        v((TILES, DEPTH, TILE), BF16),
        v((TILES, DEPTH, TILE), BF16),
        v((DEPTH, WIDE), BF16),
        v((HEADS, DEPTH), BF16),
        pltpu.SMEM((HEADS,), F32),
        pltpu.SMEM((HEADS,), F32),
        pltpu.SMEM((HEADS,), F32),
        v((LANES, DEPTH), BF16),
        v((KCONV, HEADS * LANES), F32),
        v((KCONV, WIDE), F32),
        v((1, HEADS * LANES), F32),
        v((1, HEADS * LANES), F32),
        v((1, ROWS), F32),
        v((1, ROWS), jnp.int32),
        v((1, ROWS), jnp.int32),
        v((HALO + LONGEST, TILE), F32),
        v((HALO + LONGEST, TILE), F32),
        v((HEADS, ROWS, LANES), BF16),
        v((ROWS, LANES), F32),
        v((ROWS, LANES), BF16),
        v((LANES, ROWS), F32),
        v((ROWS, ROWS), F32),
        v((HEADS, ROWS), F32),
        v((HEADS, ROWS), F32),
        v((HEADS, ROWS), F32),
        v((HEADS, ROWS), F32),
        v((HEADS, LANES), F32),
        v((PLANE, HEADS, LANES), F32),
        v((HEADS, LANES), F32),
        v((DEPTHS, HEADS, LANES), F32),
        v((HEADS, ROWS, LANES), F32),
        v((HEADS, ROWS, LANES), F32),
        v((PLANE, LANES, LANES), BF16),
        v((PLANE, LANES, LANES), BF16),
        v((PLANE, LANES, LANES), F32),
        v((PLANE, 8, LANES), F32),
        v((LANES, LANES), BF16),
        v((DEPTHS, LANES, LANES), BF16),
        v((PLANE, LANES, LANES), BF16),
        v((PLANE, LANES, LANES), BF16),
        v((ROWS, LANES), F32),
        v((ROWS, LANES), F32),
        v((2, ROWS), F32),
        v((PEERS, 2, ROWS), F32),
        v((PEERS, 2, LANES), F32),
        v((8, ROWS + LANES), F32),
        v((8, LANES), F32),
        v((16, ROWS), F32),
        v((1, LANES), F32),
        v((DEPTHS * PLANE, 1, LANES), F32),
        dma((13,)),
        dma((2, TILES)),
        dma((4,)),
        dma((7,)),
        dma((7,)),
        dma((DEPTHS,)),
        dma((DEPTHS,)),
        dma((PLANE,)),
    ]


def per_device(
    states,
    inner_weight,
    gate_weight,
    state_weight,
    step_weight,
    step_bias,
    decay_rate,
    skip_gain,
    conv_inner,
    conv_state,
    norm_gain,
    value_weight,
    rewards,
    done_flags,
    horizon,
):
    hbm = pl.BlockSpec(memory_space=pl.ANY)
    vmem = pl.BlockSpec(memory_space=pltpu.VMEM)
    seq_total = states.shape[0] * DEPTHS * PLANE
    results = (
        jax.ShapeDtypeStruct((1, ROWS), F32),
        jax.ShapeDtypeStruct((1, ROWS), F32),
        jax.ShapeDtypeStruct((1, 1), F32),
    )
    packed = pl.pallas_call(
        functools.partial(kernel, seq_total),
        out_shape=jax.ShapeDtypeStruct((3, ROWS), F32),
        in_specs=[hbm] * 15,
        out_specs=vmem,
        scratch_shapes=scratch(),
        compiler_params=pltpu.CompilerParams(
            collective_id=0, has_side_effects=True, vmem_limit_bytes=56 * 2**20
        ),
    )(
        states,
        inner_weight,
        gate_weight,
        state_weight,
        step_weight.T,
        step_bias,
        decay_rate,
        skip_gain,
        conv_inner,
        conv_state,
        norm_gain.reshape(1, -1),
        value_weight.reshape(1, -1),
        rewards.reshape(1, -1),
        done_flags.reshape(1, -1),
        horizon.reshape(1, -1),
    )
    values, targets, loss = pl.pallas_call(
        unpack,
        out_shape=results,
        in_specs=[vmem],
        out_specs=(vmem, vmem, vmem),
    )(packed)
    return values.reshape(-1), targets.reshape(-1), loss.reshape(())


def solution(mesh):
    torus = Mesh(
        mesh.devices.reshape(DEPTHS, 4, 2, mesh.shape["head"]), SEQ + ("head",)
    )
    placed = (
        P(SEQ, None),
        P(None, "head"),
        P(None, "head"),
        P(),
        P(None, "head"),
        P("head"),
        P("head"),
        P("head"),
        P(None, "head"),
        P(),
        P("head"),
        P("head"),
        P(SEQ),
        P(SEQ),
        P(SEQ),
    )
    return jax.shard_map(
        per_device, mesh=torus, in_specs=placed, out_specs=(P(SEQ), P(SEQ), P()), check_vma=False
    )
```
